256 devices in a mesh: slab: 16 (over y, x), ex: 16 (over z, core).
Axes of the slice: x: 4, y: 4, z: 8, core: 2. Of those that a mesh axis runs over, the one named last changes fastest.
Arguments:
- hidden: bfloat16 [8192, 28672], P('ex', 'slab'), may hold values from -6 to 6
- out_grad: bfloat16 [8192, 8192], P('ex', 'slab'), may hold values from -6 to 6
- lengths: int32 [64], P('ex'), may hold values from 16 to 128
- left_signs: bfloat16 [224, 2, 16, 128], P('slab'), may hold values from -1 to 1, as said below
- left_index: int32 [224, 2], P('slab'), may hold values from 0 to 3, as said below
- right_signs: bfloat16 [128, 8192], P(None, 'slab'), may hold values from -1 to 1, as said below
Outputs:
- gram: float32 [8192, 8192], P('slab', 'ex')
The draws below stay inside these ranges and needn't reach their ends.
Inputs may be any that keep to these rules, and one draw needn't show every extreme that they name: `left_index`: the 2 column blocks listed for one row block differ. `left_signs`: every entry is +1 or -1. `right_signs`: every entry is +1 or -1.
All inputs are finite; a program needn't handle non-finite values.
Results may differ from the reference program's by a relative error of at most 0.0003.
Values sent between devices are 32-bit elements; how exact they have to be, the bound alone decides.
A program may use at most 64 MiB of HBM per device.

```python
import jax
import jax.numpy as jnp
from jax import lax

D = 8192
FF = 28672
SEQ = 128
BF = 128
KB = 4
BK = 16
NNZ = 2
K2 = 128
K1 = 64
K = 8192
EXAMPLES = 64
TOKENS = 8192


def draw_left_signs(key, part):
    key = jax.random.fold_in(key, 11)
    bits = jax.random.randint(key, (FF // BF, NNZ, BK, BF), 0, 2)
    return (2 * bits - 1).astype(jnp.float32).astype(jnp.bfloat16)


def draw_right_signs(key, part):
    key = jax.random.fold_in(key, 12)
    bits = jax.random.randint(key, (K2, D), 0, 2)
    return (2 * bits - 1).astype(jnp.float32).astype(jnp.bfloat16)


def draw_left_index(key, part):
    key = jax.random.fold_in(key, 13)
    first_key, second_key = jax.random.split(key)
    first = jax.random.randint(first_key, (FF // BF, 1), 0, KB)
    offset = jax.random.randint(second_key, (FF // BF, 1), 0, KB - NNZ + 1)
    steps = lax.broadcasted_iota(jnp.int32, (FF // BF, NNZ), 1)
    spread = jnp.where(steps == 0, 0, steps + offset)
    return ((first + spread) % KB).astype(jnp.int32)


def with_ends(values, own_key, low, high):
    longest = values.shape.index(max(values.shape))
    spots = []
    for shift in (0, 1):
        where = [jax.random.randint(jax.random.fold_in(own_key, axis), (), 0, length) for axis, length in enumerate(values.shape)]
        where[longest] = (where[longest] + shift) % values.shape[longest]
        spots.append(tuple(where))
    return values.at[spots[0]].set(low).at[spots[1]].set(high)


def block_levels(own_key, dims, cuts, smallest, high):
    loudness = 1.0
    for axis_at, blocks in cuts:
        draws = jax.random.uniform(jax.random.fold_in(jax.random.fold_in(own_key, 6), axis_at), (blocks,), jnp.float32, smallest / len(cuts), high / len(cuts))
        loudness = loudness * jnp.repeat(jnp.exp(draws), dims[axis_at] // blocks).reshape((-1,) + (1,) * (len(dims) - 1 - axis_at))
    return loudness


def bell_draw(stream_key, dims, width, reach, cuts=(), held_as=jnp.bfloat16):
    loudness = block_levels(stream_key, dims, cuts, -0.22, 0.18) if cuts else 1.0
    values = jax.random.normal(stream_key, dims, jnp.float32) * width * loudness
    return jnp.minimum(jnp.maximum(values, -reach), reach).astype(held_as)


def setup_inputs(seed: int = 0) -> dict:
    key_list = jax.random.split(jax.random.key(seed), 7)
    return {
        "hidden": bell_draw(key_list[0], (TOKENS, FF), 1.0, 6.0, ((0, 16), (1, 16))),
        "out_grad": bell_draw(key_list[1], (TOKENS, D), 1.0, 6.0, ((0, 16), (1, 16))),
        "lengths": with_ends(jax.random.randint(key_list[2], (EXAMPLES,), SEQ // 8, SEQ + 1), jax.random.fold_in(key_list[2], 1), SEQ // 8, SEQ).astype(jnp.int32),
        "left_signs": draw_left_signs(jax.random.fold_in(key_list[6], 71), 0),
        "left_index": draw_left_index(jax.random.fold_in(key_list[6], 71), 0),
        "right_signs": draw_right_signs(jax.random.fold_in(key_list[6], 71), 0),
    }


def build_left(left_signs, left_index):
    onehot = (left_index[:, :, None] == jnp.arange(KB, dtype=jnp.int32)[None, None, :]).astype(jnp.bfloat16)
    dense = jnp.einsum('rnc,rnkf->rfck', onehot, left_signs, preferred_element_type=jnp.float32)
    return dense.reshape(left_signs.shape[0] * BF, KB * BK).astype(jnp.bfloat16)


def reference(hidden, out_grad, lengths, left_signs, left_index, right_signs):
    positions = lax.broadcasted_iota(jnp.int32, (EXAMPLES, SEQ), 1)
    keep = (positions < lengths[:, None]).reshape(-1, 1)
    masked = jnp.where(keep, hidden, jnp.zeros_like(hidden))
    left = build_left(left_signs, left_index)
    act_proj = jnp.dot(masked, left, preferred_element_type=jnp.float32) * (FF ** -0.5)
    grad_proj = jnp.dot(out_grad, right_signs.T, preferred_element_type=jnp.float32) * (D ** -0.5)
    features = jnp.einsum('etk,etl->ekl', act_proj.reshape(EXAMPLES, SEQ, K1), grad_proj.reshape(EXAMPLES, SEQ, K2), precision=lax.Precision.HIGHEST)
    features = features.reshape(EXAMPLES, K) * (SEQ ** -0.5)
    return jnp.dot(features.T, features, precision=lax.Precision.HIGHEST) / EXAMPLES
```

```python
import functools

import jax
import jax.numpy as jnp
from jax import lax
from jax.experimental import pallas as pl
from jax.experimental.pallas import tpu as pltpu
from jax.sharding import PartitionSpec as P

D = 8192
FF = 28672
SEQ = 128
BF = 128
KB = 4
BK = 16
K2 = 128
K1 = 64
EX_DEV = 4
PEERS = 16
ZS = 8
TOK = SEQ // EX_DEV
HALF = TOK // 2
CHUNK = TOK + HALF

MESH = pl.DeviceIdType.MESH
F32 = jnp.float32
BF16 = jnp.bfloat16
NT = (((1,), (1,)), ((), ()))
TN = (((0,), (0,)), ((), ()))


def split(x):
    high = x.astype(BF16)
    return high, (x - high.astype(F32)).astype(BF16)


def remote(src, dst, send_sem, recv_sem, slab, ex):
    return pltpu.make_async_remote_copy(
        src_ref=src,
        dst_ref=dst,
        send_sem=send_sem,
        recv_sem=recv_sem,
        device_id=(slab, ex),
        device_id_type=MESH,
    )


def wait_bytes(ref, sem):
    pltpu.make_async_copy(ref, ref, sem).wait()


def exchange(
    rows_per_block,
    hidden,
    out_grad,
    right,
    signs,
    index,
    lengths,
    a_out,
    b_out,
    hid_v,
    og_v,
    right_v,
    signs_v,
    left_v,
    part,
    part_in,
    feat,
    row_send,
    row_recv,
    col_send,
    col_recv,
    g_send,
    c_part,
    c_buf,
    r_buf,
    hid_sem,
    og_sem,
    par_sem,
    send_sem,
    recv_sem,
):
    s = lax.axis_index("slab")
    e = lax.axis_index("ex")
    y, x = s // EX_DEV, s % EX_DEV
    z, c = e // 2, e % 2
    place = c * ZS + z

    barrier = pltpu.get_barrier_semaphore()

    @pl.loop(1, PEERS)
    def _(i):
        pl.semaphore_signal(
            barrier, inc=1, device_id=(lax.rem(s + i, PEERS), e), device_id_type=MESH
        )
        pl.semaphore_signal(
            barrier, inc=1, device_id=(s, lax.rem(e + i, PEERS)), device_id_type=MESH
        )

    copies = []
    par = [
        pltpu.make_async_copy(signs, signs_v, par_sem.at[0]),
        pltpu.make_async_copy(right, right_v, par_sem.at[1]),
    ]
    for copy in par:
        copy.start()
    owners = [lax.rem(y + 1 + i, EX_DEV) for i in range(EX_DEV)]
    for i, j in enumerate(owners):
        rows = pl.ds(pl.multiple_of(j * SEQ, SEQ), SEQ)
        pair = (
            pltpu.make_async_copy(hidden.at[rows], hid_v.at[i], hid_sem.at[i]),
            pltpu.make_async_copy(out_grad.at[rows], og_v.at[i], og_sem.at[i]),
        )
        for copy in pair:
            copy.start()
        copies.append(pair)

    par[0].wait()
    for r in range(rows_per_block):
        blocks = [signs_v[r, n].astype(F32) for n in range(2)]
        for k in range(KB):
            on = [(index[r, n] == k).astype(F32) for n in range(2)]
            dense = (blocks[0] * on[0] + blocks[1] * on[1]).astype(BF16)
            cols = pl.ds(r * BF, BF)
            left_v[pl.ds(k * BK, BK), cols] = dense
            left_v[pl.ds(K1 + k * BK, BK), cols] = dense
    par[1].wait()

    lane = lax.broadcasted_iota(jnp.int32, (HALF, SEQ), 1)
    first = lane < K1
    token = lax.broadcasted_iota(jnp.int32, (SEQ, SEQ), 0)
    for i, j in enumerate(owners):
        for copy in copies[i]:
            copy.wait()
        act = lax.dot_general(hid_v[i], left_v[...], NT, preferred_element_type=F32)
        act = jnp.where(token < lengths[j], act, 0.0)
        grad = lax.dot_general(og_v[i], right_v[...], NT, preferred_element_type=F32)
        for q in range(EX_DEV):
            at = i * EX_DEV + q
            part[at, :TOK] = grad[q * TOK : (q + 1) * TOK]
            part[at, TOK:] = jnp.where(
                first,
                act[q * TOK : q * TOK + HALF],
                act[q * TOK + HALF : (q + 1) * TOK],
            )
        if i == 0:
            pl.semaphore_wait(barrier, 2 * (PEERS - 1))
        if i < EX_DEV - 1:
            for q in range(EX_DEV):
                remote(
                    part.at[i * EX_DEV + q],
                    part_in.at[s],
                    send_sem.at[0],
                    recv_sem.at[0],
                    j * EX_DEV + q,
                    e,
                ).start()
        else:
            for k in range(1, EX_DEV):
                q = lax.rem(x + k, EX_DEV)
                remote(
                    part.at[i * EX_DEV + q],
                    part_in.at[s],
                    send_sem.at[0],
                    recv_sem.at[0],
                    y * EX_DEV + q,
                    e,
                ).start()
    part_in[s] = part[(EX_DEV - 1) * EX_DEV + x]
    wait_bytes(part_in.at[pl.ds(0, PEERS - 1)], recv_sem.at[0])

    total = part_in[0]
    for i in range(1, PEERS):
        total += part_in[i]
    grad_h, grad_l = split(total[:TOK] * (D**-0.5 * SEQ**-0.5))
    packed = total[TOK:] * FF**-0.5
    acts = jnp.concatenate([jnp.where(first, packed, 0.0), jnp.where(first, 0.0, packed)], axis=0)
    act_h, act_l = split(acts)
    outer = lax.dot_general(
        jnp.concatenate([act_h, act_h, act_l, act_l], axis=0),
        jnp.concatenate([grad_h, grad_l, grad_h, grad_l], axis=0),
        TN,
        preferred_element_type=F32,
    )
    features = outer[:K1] + outer[K1:]
    feat[...] = features
    for i in range(PEERS):
        row_send[i] = features[i * EX_DEV : (i + 1) * EX_DEV]
    for m in range(EX_DEV):
        col_send[m] = feat[pl.ds(m, PEERS, stride=EX_DEV), :]

    for k in range(1, EX_DEV):
        q = lax.rem(x + k, EX_DEV)
        remote(
            col_send.at[q],
            col_recv.at[x],
            send_sem.at[1],
            recv_sem.at[1],
            y * EX_DEV + q,
            e,
        ).start()

    @pl.loop(1, PEERS)
    def _(i):
        to = lax.rem(s + i, PEERS)
        remote(row_send.at[to], row_recv.at[s], send_sem.at[2], recv_sem.at[2], to, e).start()

    col_recv[x] = col_send[x]
    row_recv[s] = row_send[s]
    wait_bytes(col_recv.at[pl.ds(0, EX_DEV - 1)], recv_sem.at[1])
    mine = col_recv[0] + col_recv[1] + col_recv[2] + col_recv[3]
    for i in range(PEERS):
        g_send[i] = mine[i : i + 1]

    @pl.loop(1, PEERS)
    def _(i):
        to = lax.rem(e + i, PEERS)
        remote(g_send.at[to], c_part.at[place], send_sem.at[3], recv_sem.at[3], s, to).start()

    c_part[place] = g_send[e]

    wait_bytes(row_recv.at[pl.ds(0, PEERS - 1)], recv_sem.at[2])
    rows = [
        row_recv[4 * j] + row_recv[4 * j + 1] + row_recv[4 * j + 2] + row_recv[4 * j + 3]
        for j in range(EX_DEV)
    ]
    own = pl.ds(pl.multiple_of(place * PEERS, PEERS), PEERS)
    r_buf[own] = jnp.concatenate(rows, axis=0)
    for k in range(1, ZS):
        to = lax.rem(z + k, ZS) * 2 + c
        remote(r_buf.at[own], r_buf.at[own], send_sem.at[4], recv_sem.at[4], s, to).start()

    wait_bytes(c_part.at[pl.ds(0, PEERS - 1)], recv_sem.at[3])
    c_buf[s] = c_part[...].reshape(PEERS, K2)

    @pl.loop(1, PEERS)
    def _(i):
        to = lax.rem(s + i, PEERS)
        remote(c_buf.at[s], c_buf.at[s], send_sem.at[5], recv_sem.at[5], to, e).start()

    seven = pl.ds(0, (ZS - 1) * PEERS)
    wait_bytes(r_buf.at[seven], recv_sem.at[4])
    side = pl.ds(pl.multiple_of(c * (ZS * PEERS), ZS * PEERS), ZS * PEERS)
    across = remote(
        r_buf.at[side], r_buf.at[side], send_sem.at[6], recv_sem.at[6], s, z * 2 + 1 - c
    )
    across.start()

    wait_bytes(c_buf.at[pl.ds(0, PEERS - 1)], recv_sem.at[5])
    cols = jnp.concatenate(
        [
            jnp.concatenate([c_buf[4 * j + m] for j in range(EX_DEV)], axis=0)
            for m in range(EX_DEV)
        ],
        axis=1,
    )
    high, low = split(cols)
    for k, piece in enumerate((high, low, high, low)):
        b_out[pl.ds(k * K1, K1)] = piece

    wait_bytes(r_buf.at[pl.ds(0, ZS * PEERS)], recv_sem.at[6])
    rows = jnp.concatenate(
        [
            jnp.concatenate(
                [r_buf[pl.ds(4 * j + m, PEERS, stride=PEERS), :] for j in range(EX_DEV)], axis=0
            )
            for m in range(EX_DEV)
        ],
        axis=1,
    )
    high, low = split(rows)
    for k, piece in enumerate((high, high, low, low)):
        a_out[pl.ds(k * K1, K1)] = piece

    wait_bytes(part.at[pl.ds(0, PEERS - 1)], send_sem.at[0])
    wait_bytes(col_send.at[pl.ds(0, EX_DEV - 1)], send_sem.at[1])
    wait_bytes(row_send.at[pl.ds(0, PEERS - 1)], send_sem.at[2])
    wait_bytes(g_send.at[pl.ds(0, PEERS - 1)], send_sem.at[3])
    wait_bytes(r_buf.at[seven], send_sem.at[4])
    wait_bytes(c_buf.at[pl.ds(0, PEERS - 1)], send_sem.at[5])
    wait_bytes(r_buf.at[pl.ds(0, ZS * PEERS)], send_sem.at[6])


def gram_block(a_ref, b_ref, out_ref):
    out_ref[...] = lax.dot_general(
        a_ref[...], b_ref[...], TN, preferred_element_type=F32
    ) * (1.0 / (PEERS * EX_DEV))


def shards(hidden, out_grad, lengths, left_signs, left_index, right_signs):
    tokens, ff = hidden.shape
    features = out_grad.shape[1]
    blocks = left_signs.shape[0]
    hbm = pl.BlockSpec(memory_space=pl.ANY)
    smem = pl.BlockSpec(memory_space=pltpu.SMEM)
    vmem = pl.BlockSpec(memory_space=pltpu.VMEM)
    wide = EX_DEV * K2
    a, b = pl.pallas_call(
        functools.partial(exchange, blocks),
        out_shape=[jax.ShapeDtypeStruct((EX_DEV * K1, wide), BF16)] * 2,
        in_specs=[hbm, hbm, hbm, hbm, smem, smem],
        out_specs=[vmem, vmem],
        scratch_shapes=[
            pltpu.VMEM((EX_DEV, SEQ, ff), BF16),
            pltpu.VMEM((EX_DEV, SEQ, features), BF16),
            pltpu.VMEM((K2, features), BF16),
            pltpu.VMEM((blocks, 2, BK, BF), BF16),
            pltpu.VMEM((2 * K1, ff), BF16),
            pltpu.VMEM((PEERS, CHUNK, SEQ), F32),
            pltpu.VMEM((PEERS, CHUNK, SEQ), F32),
            pltpu.VMEM((K1, K2), F32),
            pltpu.VMEM((PEERS, EX_DEV, K2), F32),
            pltpu.VMEM((PEERS, EX_DEV, K2), F32),
            pltpu.VMEM((EX_DEV, PEERS, K2), F32),
            pltpu.VMEM((EX_DEV, PEERS, K2), F32),
            pltpu.VMEM((PEERS, 1, K2), F32),
            pltpu.VMEM((PEERS, 1, K2), F32),
            pltpu.VMEM((PEERS, PEERS, K2), F32),
            pltpu.VMEM((PEERS * PEERS, K2), F32),
            pltpu.SemaphoreType.DMA((EX_DEV,)),
            pltpu.SemaphoreType.DMA((EX_DEV,)),
            pltpu.SemaphoreType.DMA((2,)),
            pltpu.SemaphoreType.DMA((7,)),
            pltpu.SemaphoreType.DMA((7,)),
        ],
        compiler_params=pltpu.CompilerParams(
            collective_id=0, has_side_effects=True, vmem_limit_bytes=32 * 1024 * 1024
        ),
        name="exchange",
    )(hidden, out_grad, right_signs, left_signs, left_index, lengths)
    return pl.pallas_call(
        gram_block,
        out_shape=jax.ShapeDtypeStruct((wide, wide), F32),
        in_specs=[vmem, vmem],
        out_specs=vmem,
        name="gram",
    )(a, b)


def solution(mesh):
    in_specs = (
        P("ex", "slab"),
        P("ex", "slab"),
        P("ex"),
        P("slab", None, None, None),
        P("slab", None),
        P(None, "slab"),
    )
    out_specs = P("slab", "ex")
    return jax.shard_map(shards, mesh=mesh, in_specs=in_specs, out_specs=out_specs, check_vma=False)
```

```python
import functools

import jax
import jax.numpy as jnp
from jax import lax
from jax.experimental import pallas as pl
from jax.experimental.pallas import tpu as pltpu
from jax.sharding import PartitionSpec as P

D = 8192
FF = 28672
SEQ = 128
BF = 128
KB = 4
BK = 16
K2 = 128
K1 = 64
EX_DEV = 4
PEERS = 16
ZS = 8
TOK = SEQ // 2
LANES = 128
HALF = LANES // 2
SCALE = FF**-0.5 * D**-0.5 * SEQ**-0.5

MESH = pl.DeviceIdType.MESH
F32 = jnp.float32
BF16 = jnp.bfloat16
NT = (((1,), (1,)), ((), ()))
TN = (((0,), (0,)), ((), ()))


def split(x):
    high = x.astype(BF16)
    return high, (x - high.astype(F32)).astype(BF16)


def remote(src, dst, send_sem, recv_sem, slab, ex):
    return pltpu.make_async_remote_copy(
        src_ref=src,
        dst_ref=dst,
        send_sem=send_sem,
        recv_sem=recv_sem,
        device_id=(slab, ex),
        device_id_type=MESH,
    )


def wait_bytes(ref, sem):
    pltpu.make_async_copy(ref, ref, sem).wait()


def place_halves(first, low, high):
    planes = [None] * EX_DEV
    for mm in range(2):
        planes[mm] = jnp.where(first, low[mm], pltpu.roll(high[mm], HALF, 1))
        planes[2 + mm] = jnp.where(first, pltpu.roll(low[mm], HALF, 1), high[mm])
    return jnp.concatenate(planes, axis=1)


def exchange(
    blocks,
    hidden,
    out_grad,
    right,
    signs,
    index,
    lengths,
    out,
    hid_v,
    og_v,
    right_v,
    signs_v,
    index_v,
    lengths_v,
    left_v,
    part,
    part_in,
    feat,
    row_in,
    c_buf,
    r_buf,
    hid_sem,
    og_sem,
    par_sem,
    send_sem,
    recv_sem,
):
    s = lax.axis_index("slab")
    e = lax.axis_index("ex")
    y, x = s // EX_DEV, s % EX_DEV
    low_half = s % 2 == 0

    barrier = pltpu.get_barrier_semaphore()

    @pl.loop(1, PEERS)
    def _(i):
        pl.semaphore_signal(
            barrier, inc=1, device_id=(lax.rem(s + i, PEERS), e), device_id_type=MESH
        )
        pl.semaphore_signal(
            barrier, inc=1, device_id=(s, lax.rem(e + i, PEERS)), device_id_type=MESH
        )

    par = [
        pltpu.make_async_copy(signs, signs_v, par_sem.at[0]),
        pltpu.make_async_copy(index, index_v, par_sem.at[1]),
        pltpu.make_async_copy(lengths, lengths_v, par_sem.at[2]),
        pltpu.make_async_copy(right, right_v, par_sem.at[3]),
    ]
    for copy in par:
        copy.start()
    owners = [lax.rem(y + 1 + i, EX_DEV) for i in range(EX_DEV)]
    copies = []
    for i, j in enumerate(owners):
        rows = pl.ds(pl.multiple_of(j * SEQ, SEQ), SEQ)
        pair = (
            pltpu.make_async_copy(hidden.at[rows], hid_v.at[i], hid_sem.at[i]),
            pltpu.make_async_copy(out_grad.at[rows], og_v.at[i], og_sem.at[i]),
        )
        for copy in pair:
            copy.start()
        copies.append(pair)

    par[0].wait()
    par[1].wait()
    for r in range(blocks):
        pair = [signs_v[r, n].astype(F32) for n in range(2)]
        for k in range(KB):
            on = [(index_v[n, r] == k).astype(F32) for n in range(2)]
            dense = (pair[0] * on[0] + pair[1] * on[1]).astype(BF16)
            cols = pl.ds(r * BF, BF)
            left_v[pl.ds(k * BK, BK), cols] = dense
            left_v[pl.ds(K1 + k * BK, BK), cols] = dense
    par[2].wait()
    par[3].wait()

    token = lax.broadcasted_iota(jnp.int32, (SEQ, LANES), 0)
    first = lax.broadcasted_iota(jnp.int32, (TOK, LANES), 1) < HALF
    for i, j in enumerate(owners):
        for copy in copies[i]:
            copy.wait()
        act = lax.dot_general(hid_v[i], left_v[...], NT, preferred_element_type=F32)
        act = jnp.where(token < lengths_v[j], act, 0.0)
        grad = lax.dot_general(og_v[i], right_v[...], NT, preferred_element_type=F32)
        for h in range(2):
            a, g = act[h * TOK : (h + 1) * TOK], grad[h * TOK : (h + 1) * TOK]
            part[i * EX_DEV + h * 2] = jnp.where(first, g, a)
            part[i * EX_DEV + h * 2 + 1] = jnp.where(first, a, g)
        if i == 0:
            pl.semaphore_wait(barrier, 2 * (PEERS - 1))
        for k in range(EX_DEV) if i < EX_DEV - 1 else range(1, EX_DEV):
            q = lax.rem(x + k, EX_DEV)
            remote(
                part.at[i * EX_DEV + q],
                part_in.at[s],
                send_sem.at[0],
                recv_sem.at[0],
                j * EX_DEV + q,
                e,
            ).start()
    part_in[s] = part[(EX_DEV - 1) * EX_DEV + x]
    wait_bytes(part_in.at[pl.ds(0, PEERS - 1)], recv_sem.at[0])

    total = part_in[0]
    for i in range(1, PEERS):
        total += part_in[i]
    high, low = split(total)
    outer = lax.dot_general(
        jnp.concatenate([high, high, low, low], axis=0),
        jnp.concatenate([high, low, high, low], axis=0),
        TN,
        preferred_element_type=F32,
    )
    mine = jnp.where(low_half, outer[K1:], outer[:K1]) * SCALE
    turned = pltpu.roll(mine, HALF, 1)
    lower = jnp.where(low_half, mine, turned)
    upper = jnp.where(low_half, turned, mine)
    packed = jnp.where(first, lower, pltpu.roll(upper, K1 - 2, 0))
    for i in range(PEERS):
        feat[i] = packed[i * EX_DEV : i * EX_DEV + 2]

    @pl.loop(1, PEERS)
    def _(i):
        to = lax.rem(e + i, PEERS)
        remote(feat.at[to], c_buf.at[s, e], send_sem.at[1], recv_sem.at[1], s, to).start()

    @pl.loop(1, PEERS)
    def _(i):
        to = lax.rem(s + i, PEERS)
        remote(feat.at[to], row_in.at[s], send_sem.at[2], recv_sem.at[2], to, e).start()

    c_buf[s, e] = feat[e]
    row_in[s] = feat[s]

    wait_bytes(row_in.at[pl.ds(0, PEERS - 1)], recv_sem.at[2])
    rows = [row_in[4 * j + b] + row_in[4 * j + 2 + b] for j in range(EX_DEV) for b in range(2)]
    own = pl.ds(pl.multiple_of(e * PEERS, PEERS), PEERS)
    r_buf[own] = jnp.concatenate(rows, axis=0)

    @pl.loop(1, PEERS)
    def _(i):
        to = lax.rem(e + i, PEERS)
        remote(r_buf.at[own], r_buf.at[own], send_sem.at[3], recv_sem.at[3], s, to).start()

    wait_bytes(c_buf.at[0, pl.ds(0, PEERS - 1)], recv_sem.at[1])

    @pl.loop(1, PEERS)
    def _(i):
        to = lax.rem(s + i, PEERS)
        remote(c_buf.at[s], c_buf.at[s], send_sem.at[4], recv_sem.at[4], to, e).start()

    wait_bytes(c_buf.at[pl.ds(0, PEERS - 1)], recv_sem.at[4])
    halves = []
    for b in range(2):
        sums = [c_buf[4 * j + b] + c_buf[4 * j + 2 + b] for j in range(EX_DEV)]
        halves.append([jnp.concatenate([t[:, mm] for t in sums], axis=0) for mm in range(2)])
    high, low = split(place_halves(first, *halves))
    col_side = jnp.concatenate([high, low, high, low], axis=0)

    wait_bytes(r_buf.at[pl.ds(0, (PEERS - 1) * PEERS)], recv_sem.at[3])
    halves = [
        [
            jnp.concatenate(
                [r_buf[pl.ds(4 * j + 2 * b + mm, PEERS, stride=PEERS), :] for j in range(EX_DEV)],
                axis=0,
            )
            for mm in range(2)
        ]
        for b in range(2)
    ]
    high, low = split(place_halves(first, *halves) * (1.0 / (PEERS * EX_DEV)))
    row_side = jnp.concatenate([high, high, low, low], axis=0)
    out[...] = lax.dot_general(row_side, col_side, TN, preferred_element_type=F32)

    wait_bytes(part.at[pl.ds(0, PEERS - 1)], send_sem.at[0])
    wait_bytes(feat.at[pl.ds(0, PEERS - 1)], send_sem.at[1])
    wait_bytes(feat.at[pl.ds(0, PEERS - 1)], send_sem.at[2])
    wait_bytes(r_buf.at[pl.ds(0, (PEERS - 1) * PEERS)], send_sem.at[3])
    wait_bytes(c_buf.at[pl.ds(0, PEERS - 1)], send_sem.at[4])


def shards(hidden, out_grad, lengths, left_signs, left_index, right_signs):
    tokens, ff = hidden.shape
    features = out_grad.shape[1]
    blocks = left_signs.shape[0]
    wide = EX_DEV * K2
    operands = (hidden, out_grad, right_signs, left_signs, left_index.T, lengths)
    return pl.pallas_call(
        functools.partial(exchange, blocks),
        out_shape=pltpu.VMEM((wide, wide), F32),
        in_specs=[pl.BlockSpec(memory_space=pltpu.HBM)] * 6,
        out_specs=pl.BlockSpec(memory_space=pltpu.VMEM),
        scratch_shapes=[
            pltpu.VMEM((EX_DEV, SEQ, ff), BF16),
            pltpu.VMEM((EX_DEV, SEQ, features), BF16),
            pltpu.VMEM((K2, features), BF16),
            pltpu.VMEM((blocks, 2, BK, BF), BF16),
            pltpu.SMEM((2, blocks), jnp.int32),
            pltpu.SMEM((EX_DEV,), jnp.int32),
            pltpu.VMEM((2 * K1, ff), BF16),
            pltpu.VMEM((PEERS, TOK, LANES), F32),
            pltpu.VMEM((PEERS, TOK, LANES), F32),
            pltpu.VMEM((PEERS, 2, LANES), F32),
            pltpu.VMEM((PEERS, 2, LANES), F32),
            pltpu.VMEM((PEERS, PEERS, 2, LANES), F32),
            pltpu.VMEM((PEERS * PEERS, LANES), F32),
            pltpu.SemaphoreType.DMA((EX_DEV,)),
            pltpu.SemaphoreType.DMA((EX_DEV,)),
            pltpu.SemaphoreType.DMA((4,)),
            pltpu.SemaphoreType.DMA((5,)),
            pltpu.SemaphoreType.DMA((5,)),
        ],
        compiler_params=pltpu.CompilerParams(
            collective_id=0, has_side_effects=True, vmem_limit_bytes=32 * 1024 * 1024
        ),
        name="exchange",
    )(*(pltpu.with_memory_space_constraint(a, pltpu.HBM) for a in operands))


def solution(mesh):
    in_specs = (
        P("ex", "slab"),
        P("ex", "slab"),
        P("ex"),
        P("slab", None, None, None),
        P("slab", None),
        P(None, "slab"),
    )
    out_specs = P("slab", "ex")
    return jax.shard_map(shards, mesh=mesh, in_specs=in_specs, out_specs=out_specs, check_vma=False)
```

```python
import functools

import jax
import jax.numpy as jnp
from jax import lax
from jax.experimental import pallas as pl
from jax.experimental.pallas import tpu as pltpu
from jax.sharding import PartitionSpec as P

D = 8192
FF = 28672
SEQ = 128
BF = 128
KB = 4
BK = 16
K2 = 128
K1 = 64
EX_DEV = 4
PEERS = 16
ZS = 8
NEAR = (2, 6, 1, 7)
FAR = (4, 3, 5)
Y_ORDER = (2, 1, 3, 0)
X_ORDER = (2, 1, 3, 0)
COMPUTED = 0
TOK = SEQ // 4
CHUNK = TOK + TOK // 2
LANES = 128
HALF = LANES // 2
SCALE = FF**-0.5 * D**-0.5 * SEQ**-0.5

MESH = pl.DeviceIdType.MESH
F32 = jnp.float32
BF16 = jnp.bfloat16
NT = (((1,), (1,)), ((), ()))
TN = (((0,), (0,)), ((), ()))


def split(x):
    high = x.astype(BF16)
    return high, (x - high.astype(F32)).astype(BF16)


def remote(src, dst, send_sem, recv_sem, slab, ex):
    return pltpu.make_async_remote_copy(
        src_ref=src,
        dst_ref=dst,
        send_sem=send_sem,
        recv_sem=recv_sem,
        device_id=(slab, ex),
        device_id_type=MESH,
    )


def wait_bytes(ref, sem):
    pltpu.make_async_copy(ref, ref, sem).wait()


def group_slot(g):
    return lax.rem(g, EX_DEV) * EX_DEV + lax.div(g, EX_DEV)


def gather_rows(ref, stride, step):
    planes = []
    for m in range(EX_DEV):
        rows = [ref[pl.ds(j * step + m, PEERS, stride=stride), :] for j in range(EX_DEV)]
        planes.append(jnp.concatenate(rows, axis=0))
    return jnp.concatenate(planes, axis=1)


def exchange(
    blocks,
    hidden,
    out_grad,
    right,
    signs,
    index,
    lengths,
    out,
    hid_v,
    og_v,
    right_v,
    signs_v,
    index_v,
    lengths_v,
    left_v,
    part,
    part_in,
    feat,
    row_in,
    c_in,
    c_buf,
    r_buf,
    hid_sem,
    og_sem,
    par_sem,
    send_sem,
    recv_sem,
    ready,
):
    s = lax.axis_index("slab")
    e = lax.axis_index("ex")
    y, x = lax.div(s, EX_DEV), lax.rem(s, EX_DEV)
    z, c = lax.div(e, 2), lax.rem(e, 2)

    barrier = pltpu.get_barrier_semaphore()
    for i in range(1, PEERS):
        pl.semaphore_signal(
            barrier, inc=1, device_id=(lax.rem(s + i, PEERS), e), device_id_type=MESH
        )

    @pl.loop(e + 1, PEERS)
    def _(to):
        pl.semaphore_signal(barrier, inc=1, device_id=(s, to), device_id_type=MESH)

    par = [
        pltpu.make_async_copy(signs, signs_v, par_sem.at[0]),
        pltpu.make_async_copy(index, index_v, par_sem.at[1]),
        pltpu.make_async_copy(lengths, lengths_v, par_sem.at[2]),
        pltpu.make_async_copy(right, right_v, par_sem.at[3]),
    ]
    for copy in par:
        copy.start()
    owners = [lax.rem(y + i, EX_DEV) for i in Y_ORDER]
    copies = []
    for i, j in enumerate(owners):
        rows = pl.ds(pl.multiple_of(j * SEQ, SEQ), SEQ)
        pair = (
            pltpu.make_async_copy(hidden.at[rows], hid_v.at[i], hid_sem.at[i]),
            pltpu.make_async_copy(out_grad.at[rows], og_v.at[i], og_sem.at[i]),
        )
        for copy in pair:
            copy.start()
        copies.append(pair)

    par[0].wait()
    par[1].wait()
    for r in range(blocks):
        pair = [signs_v[r, n].astype(F32) for n in range(2)]
        for k in range(KB):
            on = [(index_v[n, r] == k).astype(F32) for n in range(2)]
            dense = (pair[0] * on[0] + pair[1] * on[1]).astype(BF16)
            cols = pl.ds(r * BF, BF)
            left_v[pl.ds(k * BK, BK), cols] = dense
            left_v[pl.ds(K1 + k * BK, BK), cols] = dense
    par[2].wait()
    par[3].wait()

    token = lax.broadcasted_iota(jnp.int32, (SEQ, LANES), 0)
    first = lax.broadcasted_iota(jnp.int32, (TOK // 2, LANES), 1) < HALF
    for i, j in enumerate(owners):
        for copy in copies[i]:
            copy.wait()
        act = lax.dot_general(hid_v[i], left_v[...], NT, preferred_element_type=F32)
        act = jnp.where(token < lengths_v[j], act, 0.0)
        grad = lax.dot_general(og_v[i], right_v[...], NT, preferred_element_type=F32)
        for q in range(EX_DEV):
            at = i * EX_DEV + q
            t = q * TOK
            part[at, :TOK] = grad[t : t + TOK]
            part[at, TOK:] = jnp.where(first, act[t : t + TOK // 2], act[t + TOK // 2 : t + TOK])
        if i == COMPUTED:
            pl.semaphore_wait(barrier, PEERS - 1 + e)

            @pl.loop(0, e)
            def _(to):
                pl.semaphore_signal(ready, inc=1, device_id=(s, to), device_id_type=MESH)

        if i < COMPUTED:
            continue
        for n in range(i + 1) if i == COMPUTED else (i,):
            for k in X_ORDER:
                if Y_ORDER[n] == 0 and k == 0:
                    continue
                q = lax.rem(x + k, EX_DEV)
                remote(
                    part.at[n * EX_DEV + q],
                    part_in.at[s],
                    send_sem.at[0],
                    recv_sem.at[0],
                    owners[n] * EX_DEV + q,
                    e,
                ).start()

    part_in[s] = part[Y_ORDER.index(0) * EX_DEV + x]
    wait_bytes(part_in.at[pl.ds(0, PEERS - 1)], recv_sem.at[0])

    total = part_in[0]
    for i in range(1, PEERS):
        total += part_in[i]
    packed = total[TOK:]
    acts = jnp.concatenate([jnp.where(first, packed, 0.0), jnp.where(first, 0.0, packed)], axis=0)
    act_h, act_l = split(acts)
    grad_h, grad_l = split(total[:TOK])
    outer = lax.dot_general(
        jnp.concatenate([act_h, act_h, act_l, act_l], axis=0),
        jnp.concatenate([grad_h, grad_l, grad_h, grad_l], axis=0),
        TN,
        preferred_element_type=F32,
    )
    features = (outer[:K1] + outer[K1:]) * SCALE
    for i in range(PEERS):
        feat[i] = features[i * EX_DEV : (i + 1) * EX_DEV]

    meet = y * EX_DEV + lax.rem(e, EX_DEV)
    spot = c_in.at[x, lax.div(e, EX_DEV)]

    def give(to):
        remote(feat.at[to], spot, send_sem.at[2], recv_sem.at[2], meet, to).start()

    pl.loop(0, e)(give)

    @pl.loop(1, PEERS)
    def _(i):
        to = lax.rem(s + i, PEERS)
        remote(feat.at[to], row_in.at[s], send_sem.at[1], recv_sem.at[1], to, e).start()


    @pl.when(e < PEERS - 1)
    def _():
        pl.semaphore_wait(ready, PEERS - 1 - e)

    pl.loop(e + 1, PEERS)(give)

    @pl.when(meet != s)
    def _():
        give(e)

    @pl.when(meet == s)
    def _():
        pltpu.make_async_copy(feat.at[e], spot, recv_sem.at[2]).start()

    row_in[s] = feat[s]
    wait_bytes(row_in.at[pl.ds(0, PEERS - 1)], recv_sem.at[1])
    rows = [
        row_in[4 * j] + row_in[4 * j + 1] + row_in[4 * j + 2] + row_in[4 * j + 3]
        for j in range(EX_DEV)
    ]
    def r_slot(g):
        return r_buf.at[pl.ds(pl.multiple_of(group_slot(g) * PEERS, PEERS), PEERS)]

    own = r_slot(e)
    own[...] = jnp.concatenate(rows, axis=0)

    def pass_on(g, sem, slab, ex):
        remote(r_slot(g), r_slot(g), send_sem.at[3], recv_sem.at[sem], slab, ex).start()

    for k in FAR:
        to = lax.rem(z + k, ZS) * 2
        pass_on(e, 3, s, to + c)
        pass_on(e, 3, s, to + 1 - c)
    for k in NEAR:
        pass_on(e, 4, s, lax.rem(z + k, ZS) * 2 + c)
    pass_on(e, 5, s, 2 * z + 1 - c)

    wait_bytes(c_in, recv_sem.at[2])
    c_buf[pl.ds(pl.multiple_of(s * PEERS, PEERS), PEERS)] = jnp.concatenate(
        [c_in[0, i] + c_in[1, i] + c_in[2, i] + c_in[3, i] for i in range(EX_DEV)], axis=0
    )
    at = c_buf.at[pl.ds(pl.multiple_of(s * PEERS, PEERS), PEERS)]

    @pl.loop(1, PEERS)
    def _(i):
        to = lax.rem(s + i, PEERS)
        remote(at, at, send_sem.at[4], recv_sem.at[6], to, e).start()

    wait_bytes(r_buf.at[pl.ds(0, len(NEAR) * PEERS)], recv_sem.at[4])
    for k in NEAR:
        pass_on(lax.rem(z + k, ZS) * 2 + c, 5, s, 2 * z + 1 - c)

    wait_bytes(c_buf.at[pl.ds(0, (PEERS - 1) * PEERS)], recv_sem.at[6])
    high, low = split(gather_rows(c_buf, EX_DEV, EX_DEV * PEERS))
    col_side = jnp.concatenate([high, low, high, low], axis=0)

    wait_bytes(r_buf.at[pl.ds(0, 2 * len(FAR) * PEERS)], recv_sem.at[3])
    wait_bytes(r_buf.at[pl.ds(0, (len(NEAR) + 1) * PEERS)], recv_sem.at[5])
    high, low = split(gather_rows(r_buf, PEERS, EX_DEV) * (1.0 / (PEERS * EX_DEV)))
    row_side = jnp.concatenate([high, high, low, low], axis=0)
    out[...] = lax.dot_general(row_side, col_side, TN, preferred_element_type=F32)

    wait_bytes(part.at[pl.ds(0, PEERS - 1)], send_sem.at[0])
    wait_bytes(feat.at[pl.ds(0, PEERS - 1)], send_sem.at[1])
    wait_bytes(feat.at[pl.ds(0, PEERS - 1)], send_sem.at[2])

    @pl.when(meet != s)
    def _():
        wait_bytes(feat.at[0], send_sem.at[2])

    wait_bytes(r_buf.at[pl.ds(0, (2 * len(FAR) + 2 * len(NEAR) + 1) * PEERS)], send_sem.at[3])
    wait_bytes(c_buf.at[pl.ds(0, (PEERS - 1) * PEERS)], send_sem.at[4])


def shards(hidden, out_grad, lengths, left_signs, left_index, right_signs):
    tokens, ff = hidden.shape
    features = out_grad.shape[1]
    blocks = left_signs.shape[0]
    wide = EX_DEV * K2
    operands = (hidden, out_grad, right_signs, left_signs, left_index.T, lengths)
    return pl.pallas_call(
        functools.partial(exchange, blocks),
        out_shape=pltpu.VMEM((wide, wide), F32),
        in_specs=[pl.BlockSpec(memory_space=pltpu.HBM)] * 6,
        out_specs=pl.BlockSpec(memory_space=pltpu.VMEM),
        scratch_shapes=[
            pltpu.VMEM((EX_DEV, SEQ, ff), BF16),
            pltpu.VMEM((EX_DEV, SEQ, features), BF16),
            pltpu.VMEM((K2, features), BF16),
            pltpu.VMEM((blocks, 2, BK, BF), BF16),
            pltpu.SMEM((2, blocks), jnp.int32),
            pltpu.SMEM((EX_DEV,), jnp.int32),
            pltpu.VMEM((2 * K1, ff), BF16),
            pltpu.VMEM((PEERS, CHUNK, LANES), F32),
            pltpu.VMEM((PEERS, CHUNK, LANES), F32),
            pltpu.VMEM((PEERS, EX_DEV, K2), F32),
            pltpu.VMEM((PEERS, EX_DEV, K2), F32),
            pltpu.VMEM((EX_DEV, EX_DEV, EX_DEV, K2), F32),
            pltpu.VMEM((PEERS * PEERS, K2), F32),
            pltpu.VMEM((PEERS * PEERS, K2), F32),
            pltpu.SemaphoreType.DMA((EX_DEV,)),
            pltpu.SemaphoreType.DMA((EX_DEV,)),
            pltpu.SemaphoreType.DMA((4,)),
            pltpu.SemaphoreType.DMA((5,)),
            pltpu.SemaphoreType.DMA((7,)),
            pltpu.SemaphoreType.REGULAR,
        ],
        compiler_params=pltpu.CompilerParams(
            collective_id=0, has_side_effects=True, vmem_limit_bytes=32 * 1024 * 1024
        ),
        name="exchange",
    )(*(pltpu.with_memory_space_constraint(a, pltpu.HBM) for a in operands))


def solution(mesh):
    in_specs = (
        P("ex", "slab"),
        P("ex", "slab"),
        P("ex"),
        P("slab", None, None, None),
        P("slab", None),
        P(None, "slab"),
    )
    out_specs = P("slab", "ex")
    return jax.shard_map(shards, mesh=mesh, in_specs=in_specs, out_specs=out_specs, check_vma=False)
```

```python
import functools

import jax
import jax.numpy as jnp
from jax import lax
from jax.experimental import pallas as pl
from jax.experimental.pallas import tpu as pltpu
from jax.sharding import PartitionSpec as P

D = 8192
FF = 28672
SEQ = 128
BF = 128
KB = 4
BK = 16
K2 = 128
K1 = 64
EX_DEV = 4
PEERS = 16
ZS = 8
Z_ORDER = (4, 3, 5, 2, 6, 1, 7)
Y_ORDER = (2, 1, 3, 0)
X_ORDER = (2, 1, 3, 0)
COMPUTED = 0
TOK = SEQ // 4
CHUNK = TOK + TOK // 2
LANES = 128
HALF = LANES // 2
SCALE = FF**-0.5 * D**-0.5 * SEQ**-0.5

MESH = pl.DeviceIdType.MESH
F32 = jnp.float32
BF16 = jnp.bfloat16
NT = (((1,), (1,)), ((), ()))
TN = (((0,), (0,)), ((), ()))


def split(x):
    high = x.astype(BF16)
    return high, (x - high.astype(F32)).astype(BF16)


def remote(src, dst, send_sem, recv_sem, slab, ex):
    return pltpu.make_async_remote_copy(
        src_ref=src,
        dst_ref=dst,
        send_sem=send_sem,
        recv_sem=recv_sem,
        device_id=(slab, ex),
        device_id_type=MESH,
    )


def wait_bytes(ref, sem):
    pltpu.make_async_copy(ref, ref, sem).wait()


def gather_rows(ref, stride, step):
    planes = []
    for m in range(EX_DEV):
        rows = [ref[pl.ds(j * step + m, PEERS, stride=stride), :] for j in range(EX_DEV)]
        planes.append(jnp.concatenate(rows, axis=0))
    return jnp.concatenate(planes, axis=1)


def exchange(
    blocks,
    hidden,
    out_grad,
    right,
    signs,
    index,
    lengths,
    out,
    hid_v,
    og_v,
    right_v,
    signs_v,
    index_v,
    lengths_v,
    left_v,
    part,
    part_in,
    feat,
    row_in,
    c_in,
    c_buf,
    r_buf,
    hid_sem,
    og_sem,
    par_sem,
    send_sem,
    recv_sem,
    ready,
):
    s = lax.axis_index("slab")
    e = lax.axis_index("ex")
    y, x = lax.div(s, EX_DEV), lax.rem(s, EX_DEV)
    z, c = lax.div(e, 2), lax.rem(e, 2)

    barrier = pltpu.get_barrier_semaphore()
    for i in range(1, PEERS):
        pl.semaphore_signal(
            barrier, inc=1, device_id=(lax.rem(s + i, PEERS), e), device_id_type=MESH
        )

    @pl.loop(e + 1, PEERS)
    def _(to):
        pl.semaphore_signal(barrier, inc=1, device_id=(s, to), device_id_type=MESH)

    par = [
        pltpu.make_async_copy(signs, signs_v, par_sem.at[0]),
        pltpu.make_async_copy(index, index_v, par_sem.at[1]),
        pltpu.make_async_copy(lengths, lengths_v, par_sem.at[2]),
        pltpu.make_async_copy(right, right_v, par_sem.at[3]),
    ]
    for copy in par:
        copy.start()
    owners = [lax.rem(y + i, EX_DEV) for i in Y_ORDER]
    copies = []
    for i, j in enumerate(owners):
        rows = pl.ds(pl.multiple_of(j * SEQ, SEQ), SEQ)
        pair = (
            pltpu.make_async_copy(hidden.at[rows], hid_v.at[i], hid_sem.at[i]),
            pltpu.make_async_copy(out_grad.at[rows], og_v.at[i], og_sem.at[i]),
        )
        for copy in pair:
            copy.start()
        copies.append(pair)

    par[0].wait()
    par[1].wait()
    for r in range(blocks):
        pair = [signs_v[r, n].astype(F32) for n in range(2)]
        for k in range(KB):
            on = [(index_v[n, r] == k).astype(F32) for n in range(2)]
            dense = (pair[0] * on[0] + pair[1] * on[1]).astype(BF16)
            cols = pl.ds(r * BF, BF)
            left_v[pl.ds(k * BK, BK), cols] = dense
            left_v[pl.ds(K1 + k * BK, BK), cols] = dense
    par[2].wait()
    par[3].wait()

    token = lax.broadcasted_iota(jnp.int32, (SEQ, LANES), 0)
    first = lax.broadcasted_iota(jnp.int32, (TOK // 2, LANES), 1) < HALF
    for i, j in enumerate(owners):
        for copy in copies[i]:
            copy.wait()
        act = lax.dot_general(hid_v[i], left_v[...], NT, preferred_element_type=F32)
        act = jnp.where(token < lengths_v[j], act, 0.0)
        grad = lax.dot_general(og_v[i], right_v[...], NT, preferred_element_type=F32)
        for q in range(EX_DEV):
            at = i * EX_DEV + q
            t = q * TOK
            part[at, :TOK] = grad[t : t + TOK]
            part[at, TOK:] = jnp.where(first, act[t : t + TOK // 2], act[t + TOK // 2 : t + TOK])
        if i == COMPUTED:
            pl.semaphore_wait(barrier, PEERS - 1 + e)

            @pl.loop(0, e)
            def _(to):
                pl.semaphore_signal(ready, inc=1, device_id=(s, to), device_id_type=MESH)

        if i < COMPUTED:
            continue
        for n in range(i + 1) if i == COMPUTED else (i,):
            for k in X_ORDER:
                if Y_ORDER[n] == 0 and k == 0:
                    continue
                q = lax.rem(x + k, EX_DEV)
                remote(
                    part.at[n * EX_DEV + q],
                    part_in.at[s],
                    send_sem.at[0],
                    recv_sem.at[0],
                    owners[n] * EX_DEV + q,
                    e,
                ).start()

    part_in[s] = part[Y_ORDER.index(0) * EX_DEV + x]
    wait_bytes(part_in.at[pl.ds(0, PEERS - 1)], recv_sem.at[0])

    total = part_in[0]
    for i in range(1, PEERS):
        total += part_in[i]
    packed = total[TOK:]
    acts = jnp.concatenate([jnp.where(first, packed, 0.0), jnp.where(first, 0.0, packed)], axis=0)
    act_h, act_l = split(acts)
    grad_h, grad_l = split(total[:TOK])
    outer = lax.dot_general(
        jnp.concatenate([act_h, act_h, act_l, act_l], axis=0),
        jnp.concatenate([grad_h, grad_l, grad_h, grad_l], axis=0),
        TN,
        preferred_element_type=F32,
    )
    features = (outer[:K1] + outer[K1:]) * SCALE
    for i in range(PEERS):
        feat[i] = features[i * EX_DEV : (i + 1) * EX_DEV]

    meet = y * EX_DEV + lax.rem(e, EX_DEV)
    spot = c_in.at[x, lax.div(e, EX_DEV)]

    def give(to):
        remote(feat.at[to], spot, send_sem.at[2], recv_sem.at[2], meet, to).start()

    pl.loop(0, e)(give)

    @pl.loop(1, PEERS)
    def _(i):
        to = lax.rem(s + i, PEERS)
        remote(feat.at[to], row_in.at[s], send_sem.at[1], recv_sem.at[1], to, e).start()


    @pl.when(e < PEERS - 1)
    def _():
        pl.semaphore_wait(ready, PEERS - 1 - e)

    pl.loop(e + 1, PEERS)(give)

    @pl.when(meet != s)
    def _():
        give(e)

    @pl.when(meet == s)
    def _():
        pltpu.make_async_copy(feat.at[e], spot, recv_sem.at[2]).start()

    row_in[s] = feat[s]
    wait_bytes(row_in.at[pl.ds(0, PEERS - 1)], recv_sem.at[1])
    rows = [
        row_in[4 * j] + row_in[4 * j + 1] + row_in[4 * j + 2] + row_in[4 * j + 3]
        for j in range(EX_DEV)
    ]
    slot = lax.rem(e, EX_DEV) * EX_DEV + lax.div(e, EX_DEV)
    own = r_buf.at[pl.ds(pl.multiple_of(slot * PEERS, PEERS), PEERS)]
    own[...] = jnp.concatenate(rows, axis=0)

    def pass_on(ex):
        remote(own, own, send_sem.at[3], recv_sem.at[3], s, ex).start()

    for k in Z_ORDER:
        to = lax.rem(z + k, ZS) * 2
        pass_on(to + c)
        pass_on(to + 1 - c)
    pass_on(2 * z + 1 - c)

    wait_bytes(c_in, recv_sem.at[2])
    c_buf[pl.ds(pl.multiple_of(s * PEERS, PEERS), PEERS)] = jnp.concatenate(
        [c_in[0, i] + c_in[1, i] + c_in[2, i] + c_in[3, i] for i in range(EX_DEV)], axis=0
    )
    at = c_buf.at[pl.ds(pl.multiple_of(s * PEERS, PEERS), PEERS)]

    @pl.loop(1, PEERS)
    def _(i):
        to = lax.rem(s + i, PEERS)
        remote(at, at, send_sem.at[4], recv_sem.at[4], to, e).start()


    wait_bytes(r_buf.at[pl.ds(0, (PEERS - 1) * PEERS)], recv_sem.at[3])
    high, low = split(gather_rows(r_buf, PEERS, EX_DEV) * (1.0 / (PEERS * EX_DEV)))
    row_side = jnp.concatenate([high, high, low, low], axis=0)
    wait_bytes(c_buf.at[pl.ds(0, (PEERS - 1) * PEERS)], recv_sem.at[4])
    high, low = split(gather_rows(c_buf, EX_DEV, EX_DEV * PEERS))
    col_side = jnp.concatenate([high, low, high, low], axis=0)

    out[...] = lax.dot_general(row_side, col_side, TN, preferred_element_type=F32)

    wait_bytes(part.at[pl.ds(0, PEERS - 1)], send_sem.at[0])
    wait_bytes(feat.at[pl.ds(0, PEERS - 1)], send_sem.at[1])
    wait_bytes(feat.at[pl.ds(0, PEERS - 1)], send_sem.at[2])

    @pl.when(meet != s)
    def _():
        wait_bytes(feat.at[0], send_sem.at[2])

    wait_bytes(r_buf.at[pl.ds(0, (PEERS - 1) * PEERS)], send_sem.at[3])
    wait_bytes(c_buf.at[pl.ds(0, (PEERS - 1) * PEERS)], send_sem.at[4])


def shards(hidden, out_grad, lengths, left_signs, left_index, right_signs):
    tokens, ff = hidden.shape
    features = out_grad.shape[1]
    blocks = left_signs.shape[0]
    wide = EX_DEV * K2
    operands = (hidden, out_grad, right_signs, left_signs, left_index.T, lengths)
    return pl.pallas_call(
        functools.partial(exchange, blocks),
        out_shape=pltpu.VMEM((wide, wide), F32),
        in_specs=[pl.BlockSpec(memory_space=pltpu.HBM)] * 6,
        out_specs=pl.BlockSpec(memory_space=pltpu.VMEM),
        scratch_shapes=[
            pltpu.VMEM((EX_DEV, SEQ, ff), BF16),
            pltpu.VMEM((EX_DEV, SEQ, features), BF16),
            pltpu.VMEM((K2, features), BF16),
            pltpu.VMEM((blocks, 2, BK, BF), BF16),
            pltpu.SMEM((2, blocks), jnp.int32),
            pltpu.SMEM((EX_DEV,), jnp.int32),
            pltpu.VMEM((2 * K1, ff), BF16),
            pltpu.VMEM((PEERS, CHUNK, LANES), F32),
            pltpu.VMEM((PEERS, CHUNK, LANES), F32),
            pltpu.VMEM((PEERS, EX_DEV, K2), F32),
            pltpu.VMEM((PEERS, EX_DEV, K2), F32),
            pltpu.VMEM((EX_DEV, EX_DEV, EX_DEV, K2), F32),
            pltpu.VMEM((PEERS * PEERS, K2), F32),
            pltpu.VMEM((PEERS * PEERS, K2), F32),
            pltpu.SemaphoreType.DMA((EX_DEV,)),
            pltpu.SemaphoreType.DMA((EX_DEV,)),
            pltpu.SemaphoreType.DMA((4,)),
            pltpu.SemaphoreType.DMA((5,)),
            pltpu.SemaphoreType.DMA((5,)),
            pltpu.SemaphoreType.REGULAR,
        ],
        compiler_params=pltpu.CompilerParams(
            collective_id=0, has_side_effects=True, vmem_limit_bytes=32 * 1024 * 1024
        ),
        name="exchange",
    )(*(pltpu.with_memory_space_constraint(a, pltpu.HBM) for a in operands))


def solution(mesh):
    in_specs = (
        P("ex", "slab"),
        P("ex", "slab"),
        P("ex"),
        P("slab", None, None, None),
        P("slab", None),
        P(None, "slab"),
    )
    out_specs = P("slab", "ex")
    return jax.shard_map(shards, mesh=mesh, in_specs=in_specs, out_specs=out_specs, check_vma=False)
```

```python
import functools

import jax
import jax.numpy as jnp
from jax import lax
from jax.experimental import pallas as pl
from jax.experimental.pallas import tpu as pltpu
from jax.sharding import PartitionSpec as P

D = 8192
FF = 28672
SEQ = 128
BF = 128
KB = 4
BK = 16
K2 = 128
K1 = 64
EX_DEV = 4
PEERS = 16
ZS = 8
Z_ORDER = (4, 3, 5, 2, 6, 1, 7)
Y_ORDER = (2, 3, 1, 0)
LEAD = (0, 1)
X_ORDER = (2, 1, 3, 0)
COMPUTED = 0
TOK = SEQ // 4
CHUNK = TOK + TOK // 2
LANES = 128
HALF = LANES // 2
SCALE = FF**-0.5 * D**-0.5 * SEQ**-0.5

MESH = pl.DeviceIdType.MESH
F32 = jnp.float32
BF16 = jnp.bfloat16
NT = (((1,), (1,)), ((), ()))
TN = (((0,), (0,)), ((), ()))


def split(x):
    high = x.astype(BF16)
    return high, (x - high.astype(F32)).astype(BF16)


def remote(src, dst, send_sem, recv_sem, slab, ex):
    return pltpu.make_async_remote_copy(
        src_ref=src,
        dst_ref=dst,
        send_sem=send_sem,
        recv_sem=recv_sem,
        device_id=(slab, ex),
        device_id_type=MESH,
    )


def wait_bytes(ref, sem):
    pltpu.make_async_copy(ref, ref, sem).wait()


def gather_rows(ref, stride, step):
    planes = []
    for m in range(EX_DEV):
        rows = [ref[pl.ds(j * step + m, PEERS, stride=stride), :] for j in range(EX_DEV)]
        planes.append(jnp.concatenate(rows, axis=0))
    return jnp.concatenate(planes, axis=1)


def add_quarters(ref):
    planes = [[] for _ in range(EX_DEV)]
    for j in range(EX_DEV):
        at = [ref[pl.ds((EX_DEV * j + q) * PEERS, PEERS)] for q in range(EX_DEV)]
        total = at[0] + at[1] + at[2] + at[3]
        for m in range(EX_DEV):
            planes[m].append(total[:, m])
    return jnp.concatenate([jnp.concatenate(rows, axis=0) for rows in planes], axis=1)


def exchange(
    blocks,
    hidden,
    out_grad,
    right,
    signs,
    index,
    lengths,
    out,
    hid_v,
    og_v,
    right_v,
    signs_v,
    index_v,
    lengths_v,
    left_v,
    part,
    part_in,
    feat,
    row_in,
    c_in,
    c_buf,
    r_buf,
    lead_in,
    hid_sem,
    og_sem,
    par_sem,
    send_sem,
    recv_sem,
    ready,
):
    s = lax.axis_index("slab")
    e = lax.axis_index("ex")
    y, x = lax.div(s, EX_DEV), lax.rem(s, EX_DEV)
    z, c = lax.div(e, 2), lax.rem(e, 2)

    def is_lead(slab, ex):
        return jnp.logical_and(slab == LEAD[0], ex == LEAD[1])

    lead = is_lead(s, e)

    barrier = pltpu.get_barrier_semaphore()
    for i in range(1, PEERS):
        pl.semaphore_signal(
            barrier, inc=1, device_id=(lax.rem(s + i, PEERS), e), device_id_type=MESH
        )

    @pl.loop(e + 1, PEERS)
    def _(to):
        pl.semaphore_signal(barrier, inc=1, device_id=(s, to), device_id_type=MESH)

    par = [
        pltpu.make_async_copy(signs, signs_v, par_sem.at[0]),
        pltpu.make_async_copy(index, index_v, par_sem.at[1]),
        pltpu.make_async_copy(lengths, lengths_v, par_sem.at[2]),
        pltpu.make_async_copy(right, right_v, par_sem.at[3]),
    ]
    for copy in par:
        copy.start()
    owners = [lax.rem(y + i, EX_DEV) for i in Y_ORDER]
    copies = []
    for i, j in enumerate(owners):
        rows = pl.ds(pl.multiple_of(j * SEQ, SEQ), SEQ)
        pair = (
            pltpu.make_async_copy(hidden.at[rows], hid_v.at[i], hid_sem.at[i]),
            pltpu.make_async_copy(out_grad.at[rows], og_v.at[i], og_sem.at[i]),
        )
        for copy in pair:
            copy.start()
        copies.append(pair)

    par[0].wait()
    par[1].wait()
    for r in range(blocks):
        pair = [signs_v[r, n].astype(F32) for n in range(2)]
        for k in range(KB):
            on = [(index_v[n, r] == k).astype(F32) for n in range(2)]
            dense = (pair[0] * on[0] + pair[1] * on[1]).astype(BF16)
            cols = pl.ds(r * BF, BF)
            left_v[pl.ds(k * BK, BK), cols] = dense
            left_v[pl.ds(K1 + k * BK, BK), cols] = dense
    par[2].wait()
    par[3].wait()

    token = lax.broadcasted_iota(jnp.int32, (SEQ, LANES), 0)
    first = lax.broadcasted_iota(jnp.int32, (TOK // 2, LANES), 1) < HALF
    for i, j in enumerate(owners):
        for copy in copies[i]:
            copy.wait()
        act = lax.dot_general(hid_v[i], left_v[...], NT, preferred_element_type=F32)
        act = jnp.where(token < lengths_v[j], act, 0.0)
        grad = lax.dot_general(og_v[i], right_v[...], NT, preferred_element_type=F32)
        for q in range(EX_DEV):
            at = i * EX_DEV + q
            t = q * TOK
            part[at, :TOK] = grad[t : t + TOK]
            part[at, TOK:] = jnp.where(first, act[t : t + TOK // 2], act[t + TOK // 2 : t + TOK])
        if i == COMPUTED:
            pl.semaphore_wait(barrier, PEERS - 1 + e)

            @pl.loop(0, e)
            def _(to):
                pl.semaphore_signal(ready, inc=1, device_id=(s, to), device_id_type=MESH)

        if i < COMPUTED:
            continue
        for n in range(i + 1) if i == COMPUTED else (i,):
            for k in X_ORDER:
                if Y_ORDER[n] == 0 and k == 0:
                    continue
                q = lax.rem(x + k, EX_DEV)
                remote(
                    part.at[n * EX_DEV + q],
                    part_in.at[s],
                    send_sem.at[0],
                    recv_sem.at[0],
                    owners[n] * EX_DEV + q,
                    e,
                ).start()

    part_in[s] = part[Y_ORDER.index(0) * EX_DEV + x]
    wait_bytes(part_in.at[pl.ds(0, PEERS - 1)], recv_sem.at[0])

    total = part_in[0]
    for i in range(1, PEERS):
        total += part_in[i]
    packed = total[TOK:]
    acts = jnp.concatenate([jnp.where(first, packed, 0.0), jnp.where(first, 0.0, packed)], axis=0)
    act_h, act_l = split(acts)
    grad_h, grad_l = split(total[:TOK])
    outer = lax.dot_general(
        jnp.concatenate([act_h, act_h, act_l, act_l], axis=0),
        jnp.concatenate([grad_h, grad_l, grad_h, grad_l], axis=0),
        TN,
        preferred_element_type=F32,
    )
    features = (outer[:K1] + outer[K1:]) * SCALE
    for i in range(PEERS):
        feat[i] = features[i * EX_DEV : (i + 1) * EX_DEV]

    def to_lead():
        for k in range(2):
            remote(
                feat.at[LEAD[k]],
                lead_in.at[k, s * PEERS + e],
                send_sem.at[5],
                recv_sem.at[5 + k],
                *LEAD,
            ).start()

    pl.when(e > LEAD[1])(to_lead)

    meet = y * EX_DEV + lax.rem(e, EX_DEV)
    spot = c_in.at[x, lax.div(e, EX_DEV)]

    def give(to):
        remote(feat.at[to], spot, send_sem.at[2], recv_sem.at[2], meet, to).start()

    pl.loop(0, e)(give)

    @pl.loop(1, PEERS)
    def _(i):
        to = lax.rem(s + i, PEERS)
        remote(feat.at[to], row_in.at[s], send_sem.at[1], recv_sem.at[1], to, e).start()


    @pl.when(e < PEERS - 1)
    def _():
        pl.semaphore_wait(ready, PEERS - 1 - e)

    @pl.when(jnp.logical_and(e <= LEAD[1], jnp.logical_not(lead)))
    def _():
        to_lead()

    @pl.when(lead)
    def _():
        for k in range(2):
            lead_in[k, LEAD[0] * PEERS + LEAD[1]] = feat[LEAD[k]]

    pl.loop(e + 1, PEERS)(give)

    @pl.when(meet != s)
    def _():
        give(e)

    @pl.when(meet == s)
    def _():
        pltpu.make_async_copy(feat.at[e], spot, recv_sem.at[2]).start()

    row_in[s] = feat[s]
    wait_bytes(row_in.at[pl.ds(0, PEERS - 1)], recv_sem.at[1])
    rows = [
        row_in[4 * j] + row_in[4 * j + 1] + row_in[4 * j + 2] + row_in[4 * j + 3]
        for j in range(EX_DEV)
    ]
    slot = lax.rem(e, EX_DEV) * EX_DEV + lax.div(e, EX_DEV)
    own = r_buf.at[pl.ds(pl.multiple_of(slot * PEERS, PEERS), PEERS)]
    own[...] = jnp.concatenate(rows, axis=0)

    def pass_on(ex):
        @pl.when(jnp.logical_not(is_lead(s, ex)))
        def _():
            remote(own, own, send_sem.at[3], recv_sem.at[3], s, ex).start()

    for k in Z_ORDER:
        to = lax.rem(z + k, ZS) * 2
        pass_on(to + c)
        pass_on(to + 1 - c)
    pass_on(2 * z + 1 - c)

    wait_bytes(c_in, recv_sem.at[2])
    c_buf[pl.ds(pl.multiple_of(s * PEERS, PEERS), PEERS)] = jnp.concatenate(
        [c_in[0, i] + c_in[1, i] + c_in[2, i] + c_in[3, i] for i in range(EX_DEV)], axis=0
    )
    at = c_buf.at[pl.ds(pl.multiple_of(s * PEERS, PEERS), PEERS)]

    @pl.loop(1, PEERS)
    def _(i):
        to = lax.rem(s + i, PEERS)

        @pl.when(jnp.logical_not(is_lead(to, e)))
        def _():
            remote(at, at, send_sem.at[4], recv_sem.at[4], to, e).start()


    def gram(row_side, wait, cols):
        high, low = split(row_side * (1.0 / (PEERS * EX_DEV)))
        row_side = jnp.concatenate([high, high, low, low], axis=0)
        wait()
        high, low = split(cols())
        col_side = jnp.concatenate([high, low, high, low], axis=0)
        out[...] = lax.dot_general(row_side, col_side, TN, preferred_element_type=F32)

    @pl.when(jnp.logical_not(lead))
    def _():
        wait_bytes(r_buf.at[pl.ds(0, (PEERS - 1) * PEERS)], recv_sem.at[3])
        gram(
            gather_rows(r_buf, PEERS, EX_DEV),
            lambda: wait_bytes(c_buf.at[pl.ds(0, (PEERS - 1) * PEERS)], recv_sem.at[4]),
            lambda: gather_rows(c_buf, EX_DEV, EX_DEV * PEERS),
        )

    @pl.when(lead)
    def _():
        def arrive(k):
            wait_bytes(lead_in.at[k, pl.ds(0, PEERS * PEERS - 1)], recv_sem.at[5 + k])

        arrive(0)
        gram(add_quarters(lead_in.at[0]), lambda: arrive(1), lambda: add_quarters(lead_in.at[1]))

    wait_bytes(part.at[pl.ds(0, PEERS - 1)], send_sem.at[0])
    wait_bytes(feat.at[pl.ds(0, PEERS - 1)], send_sem.at[1])
    wait_bytes(feat.at[pl.ds(0, PEERS - 1)], send_sem.at[2])

    @pl.when(meet != s)
    def _():
        wait_bytes(feat.at[0], send_sem.at[2])

    wait_bytes(r_buf.at[pl.ds(0, (PEERS - 2) * PEERS)], send_sem.at[3])
    wait_bytes(c_buf.at[pl.ds(0, (PEERS - 2) * PEERS)], send_sem.at[4])

    @pl.when(jnp.logical_or(s != LEAD[0], lead))
    def _():
        wait_bytes(r_buf.at[pl.ds(0, PEERS)], send_sem.at[3])

    @pl.when(jnp.logical_or(e != LEAD[1], lead))
    def _():
        wait_bytes(c_buf.at[pl.ds(0, PEERS)], send_sem.at[4])

    @pl.when(jnp.logical_not(lead))
    def _():
        wait_bytes(lead_in.at[0, pl.ds(0, 2)], send_sem.at[5])


def shards(hidden, out_grad, lengths, left_signs, left_index, right_signs):
    tokens, ff = hidden.shape
    features = out_grad.shape[1]
    blocks = left_signs.shape[0]
    wide = EX_DEV * K2
    operands = (hidden, out_grad, right_signs, left_signs, left_index.T, lengths)
    return pl.pallas_call(
        functools.partial(exchange, blocks),
        out_shape=pltpu.VMEM((wide, wide), F32),
        in_specs=[pl.BlockSpec(memory_space=pltpu.HBM)] * 6,
        out_specs=pl.BlockSpec(memory_space=pltpu.VMEM),
        scratch_shapes=[
            pltpu.VMEM((EX_DEV, SEQ, ff), BF16),
            pltpu.VMEM((EX_DEV, SEQ, features), BF16),
            pltpu.VMEM((K2, features), BF16),
            pltpu.VMEM((blocks, 2, BK, BF), BF16),
            pltpu.SMEM((2, blocks), jnp.int32),
            pltpu.SMEM((EX_DEV,), jnp.int32),
            pltpu.VMEM((2 * K1, ff), BF16),
            pltpu.VMEM((PEERS, CHUNK, LANES), F32),
            pltpu.VMEM((PEERS, CHUNK, LANES), F32),
            pltpu.VMEM((PEERS, EX_DEV, K2), F32),
            pltpu.VMEM((PEERS, EX_DEV, K2), F32),
            pltpu.VMEM((EX_DEV, EX_DEV, EX_DEV, K2), F32),
            pltpu.VMEM((PEERS * PEERS, K2), F32),
            pltpu.VMEM((PEERS * PEERS, K2), F32),
            pltpu.VMEM((2, PEERS * PEERS, EX_DEV, K2), F32),
            pltpu.SemaphoreType.DMA((EX_DEV,)),
            pltpu.SemaphoreType.DMA((EX_DEV,)),
            pltpu.SemaphoreType.DMA((4,)),
            pltpu.SemaphoreType.DMA((6,)),
            pltpu.SemaphoreType.DMA((7,)),
            pltpu.SemaphoreType.REGULAR,
        ],
        compiler_params=pltpu.CompilerParams(
            collective_id=0, has_side_effects=True, vmem_limit_bytes=32 * 1024 * 1024
        ),
        name="exchange",
    )(*(pltpu.with_memory_space_constraint(a, pltpu.HBM) for a in operands))


def solution(mesh):
    in_specs = (
        P("ex", "slab"),
        P("ex", "slab"),
        P("ex"),
        P("slab", None, None, None),
        P("slab", None),
        P(None, "slab"),
    )
    out_specs = P("slab", "ex")
    return jax.shard_map(shards, mesh=mesh, in_specs=in_specs, out_specs=out_specs, check_vma=False)
```

```python
import functools

import jax
import jax.numpy as jnp
from jax import lax
from jax.experimental import pallas as pl
from jax.experimental.pallas import tpu as pltpu
from jax.sharding import PartitionSpec as P

D = 8192
FF = 28672
SEQ = 128
BF = 128
KB = 4
BK = 16
K2 = 128
K1 = 64
EX_DEV = 4
PEERS = 16
ZS = 8
Z_ORDER = (4, 3, 5, 2, 6, 1, 7)
Y_ORDER = (2, 3, 1, 0)
LEADS = ((1, 3), (0, 1), (0, 1), (0, 0), (0, 1))
X_ORDER = (2, 1, 3, 0)
COMPUTED = 0
TOK = SEQ // 4
CHUNK = TOK + TOK // 2
LANES = 128
HALF = LANES // 2
SCALE = FF**-0.5 * D**-0.5 * SEQ**-0.5

MESH = pl.DeviceIdType.MESH
F32 = jnp.float32
BF16 = jnp.bfloat16
NT = (((1,), (1,)), ((), ()))
TN = (((0,), (0,)), ((), ()))


def split(x):
    high = x.astype(BF16)
    return high, (x - high.astype(F32)).astype(BF16)


def remote(src, dst, send_sem, recv_sem, slab, ex):
    return pltpu.make_async_remote_copy(
        src_ref=src,
        dst_ref=dst,
        send_sem=send_sem,
        recv_sem=recv_sem,
        device_id=(slab, ex),
        device_id_type=MESH,
    )


def wait_bytes(ref, sem):
    pltpu.make_async_copy(ref, ref, sem).wait()


def gather_rows(ref, stride, step):
    planes = []
    for m in range(EX_DEV):
        rows = [ref[pl.ds(j * step + m, PEERS, stride=stride), :] for j in range(EX_DEV)]
        planes.append(jnp.concatenate(rows, axis=0))
    return jnp.concatenate(planes, axis=1)


def leads_of(slab):
    low = high = jnp.int32(0)
    for k, (first, last) in enumerate(LEADS):
        low = jnp.where(slab == k, first, low)
        high = jnp.where(slab == k, last, high)
    return low, high


def within(ex, limits):
    return jnp.logical_and(ex >= limits[0], ex < limits[1])


def add_quarters(ref):
    planes = [[] for _ in range(EX_DEV)]
    for j in range(EX_DEV):
        at = [ref[pl.ds((EX_DEV * j + q) * PEERS, PEERS)] for q in range(EX_DEV)]
        total = at[0] + at[1] + at[2] + at[3]
        for m in range(EX_DEV):
            planes[m].append(total[:, m])
    return jnp.concatenate([jnp.concatenate(rows, axis=0) for rows in planes], axis=1)


def exchange(
    blocks,
    hidden,
    out_grad,
    right,
    signs,
    index,
    lengths,
    out,
    hid_v,
    og_v,
    right_v,
    signs_v,
    index_v,
    lengths_v,
    left_v,
    part,
    part_in,
    feat,
    row_in,
    c_in,
    c_buf,
    r_buf,
    lead_in,
    hid_sem,
    og_sem,
    par_sem,
    send_sem,
    recv_sem,
    ready,
):
    s = lax.axis_index("slab")
    e = lax.axis_index("ex")
    y, x = lax.div(s, EX_DEV), lax.rem(s, EX_DEV)
    z, c = lax.div(e, 2), lax.rem(e, 2)

    row_leads = leads_of(s)
    lead = within(e, row_leads)

    barrier = pltpu.get_barrier_semaphore()
    for i in range(1, PEERS):
        pl.semaphore_signal(
            barrier, inc=1, device_id=(lax.rem(s + i, PEERS), e), device_id_type=MESH
        )

    @pl.loop(e + 1, PEERS)
    def _(to):
        pl.semaphore_signal(barrier, inc=1, device_id=(s, to), device_id_type=MESH)

    par = [
        pltpu.make_async_copy(signs, signs_v, par_sem.at[0]),
        pltpu.make_async_copy(index, index_v, par_sem.at[1]),
        pltpu.make_async_copy(lengths, lengths_v, par_sem.at[2]),
        pltpu.make_async_copy(right, right_v, par_sem.at[3]),
    ]
    for copy in par:
        copy.start()
    owners = [lax.rem(y + i, EX_DEV) for i in Y_ORDER]
    copies = []
    for i, j in enumerate(owners):
        rows = pl.ds(pl.multiple_of(j * SEQ, SEQ), SEQ)
        pair = (
            pltpu.make_async_copy(hidden.at[rows], hid_v.at[i], hid_sem.at[i]),
            pltpu.make_async_copy(out_grad.at[rows], og_v.at[i], og_sem.at[i]),
        )
        for copy in pair:
            copy.start()
        copies.append(pair)

    par[0].wait()
    par[1].wait()
    for r in range(blocks):
        pair = [signs_v[r, n].astype(F32) for n in range(2)]
        for k in range(KB):
            on = [(index_v[n, r] == k).astype(F32) for n in range(2)]
            dense = (pair[0] * on[0] + pair[1] * on[1]).astype(BF16)
            cols = pl.ds(r * BF, BF)
            left_v[pl.ds(k * BK, BK), cols] = dense
            left_v[pl.ds(K1 + k * BK, BK), cols] = dense
    par[2].wait()
    par[3].wait()

    token = lax.broadcasted_iota(jnp.int32, (SEQ, LANES), 0)
    first = lax.broadcasted_iota(jnp.int32, (TOK // 2, LANES), 1) < HALF
    for i, j in enumerate(owners):
        for copy in copies[i]:
            copy.wait()
        act = lax.dot_general(hid_v[i], left_v[...], NT, preferred_element_type=F32)
        act = jnp.where(token < lengths_v[j], act, 0.0)
        grad = lax.dot_general(og_v[i], right_v[...], NT, preferred_element_type=F32)
        for q in range(EX_DEV):
            at = i * EX_DEV + q
            t = q * TOK
            part[at, :TOK] = grad[t : t + TOK]
            part[at, TOK:] = jnp.where(first, act[t : t + TOK // 2], act[t + TOK // 2 : t + TOK])
        if i == COMPUTED:
            pl.semaphore_wait(barrier, PEERS - 1 + e)

            @pl.loop(0, e)
            def _(to):
                pl.semaphore_signal(ready, inc=1, device_id=(s, to), device_id_type=MESH)

        if i < COMPUTED:
            continue
        for n in range(i + 1) if i == COMPUTED else (i,):
            for k in X_ORDER:
                if Y_ORDER[n] == 0 and k == 0:
                    continue
                q = lax.rem(x + k, EX_DEV)
                remote(
                    part.at[n * EX_DEV + q],
                    part_in.at[s],
                    send_sem.at[0],
                    recv_sem.at[0],
                    owners[n] * EX_DEV + q,
                    e,
                ).start()

    part_in[s] = part[Y_ORDER.index(0) * EX_DEV + x]
    wait_bytes(part_in.at[pl.ds(0, PEERS - 1)], recv_sem.at[0])

    total = part_in[0]
    for i in range(1, PEERS):
        total += part_in[i]
    packed = total[TOK:]
    acts = jnp.concatenate([jnp.where(first, packed, 0.0), jnp.where(first, 0.0, packed)], axis=0)
    act_h, act_l = split(acts)
    grad_h, grad_l = split(total[:TOK])
    outer = lax.dot_general(
        jnp.concatenate([act_h, act_h, act_l, act_l], axis=0),
        jnp.concatenate([grad_h, grad_l, grad_h, grad_l], axis=0),
        TN,
        preferred_element_type=F32,
    )
    features = (outer[:K1] + outer[K1:]) * SCALE
    for i in range(PEERS):
        feat[i] = features[i * EX_DEV : (i + 1) * EX_DEV]

    def to_leads(slabs):
        for k in slabs:
            limits = LEADS[k]

            @pl.loop(*limits)
            def _(to):
                @pl.when(jnp.logical_or(s != k, e != to))
                def _():
                    for side, at in enumerate((k, to)):
                        remote(
                            feat.at[at],
                            lead_in.at[side, s * PEERS + e],
                            send_sem.at[5],
                            recv_sem.at[5 + side],
                            k,
                            to,
                        ).start()

    @pl.when(e >= PEERS // 2)
    def _():
        to_leads((0,))

    meet = y * EX_DEV + lax.rem(e, EX_DEV)
    spot = c_in.at[x, lax.div(e, EX_DEV)]

    def give(to):
        remote(feat.at[to], spot, send_sem.at[2], recv_sem.at[2], meet, to).start()

    pl.loop(0, e)(give)

    @pl.loop(1, PEERS)
    def _(i):
        to = lax.rem(s + i, PEERS)
        remote(feat.at[to], row_in.at[s], send_sem.at[1], recv_sem.at[1], to, e).start()


    @pl.when(e < PEERS - 1)
    def _():
        pl.semaphore_wait(ready, PEERS - 1 - e)

    pl.loop(e + 1, PEERS)(give)

    @pl.when(meet != s)
    def _():
        give(e)

    @pl.when(meet == s)
    def _():
        pltpu.make_async_copy(feat.at[e], spot, recv_sem.at[2]).start()

    @pl.when(e < PEERS // 2)
    def _():
        to_leads((0,))

    to_leads(range(1, len(LEADS)))

    @pl.when(lead)
    def _():
        lead_in[0, s * PEERS + e] = feat[s]
        lead_in[1, s * PEERS + e] = feat[e]

    row_in[s] = feat[s]
    wait_bytes(row_in.at[pl.ds(0, PEERS - 1)], recv_sem.at[1])
    rows = [
        row_in[4 * j] + row_in[4 * j + 1] + row_in[4 * j + 2] + row_in[4 * j + 3]
        for j in range(EX_DEV)
    ]
    slot = lax.rem(e, EX_DEV) * EX_DEV + lax.div(e, EX_DEV)
    own = r_buf.at[pl.ds(pl.multiple_of(slot * PEERS, PEERS), PEERS)]
    own[...] = jnp.concatenate(rows, axis=0)

    def pass_on(ex):
        @pl.when(jnp.logical_not(within(ex, row_leads)))
        def _():
            remote(own, own, send_sem.at[3], recv_sem.at[3], s, ex).start()

    for k in Z_ORDER:
        to = lax.rem(z + k, ZS) * 2
        pass_on(to + c)
        pass_on(to + 1 - c)
    pass_on(2 * z + 1 - c)

    wait_bytes(c_in, recv_sem.at[2])
    c_buf[pl.ds(pl.multiple_of(s * PEERS, PEERS), PEERS)] = jnp.concatenate(
        [c_in[0, i] + c_in[1, i] + c_in[2, i] + c_in[3, i] for i in range(EX_DEV)], axis=0
    )
    at = c_buf.at[pl.ds(pl.multiple_of(s * PEERS, PEERS), PEERS)]

    @pl.loop(1, PEERS)
    def _(i):
        to = lax.rem(s + i, PEERS)

        @pl.when(jnp.logical_not(within(e, leads_of(to))))
        def _():
            remote(at, at, send_sem.at[4], recv_sem.at[4], to, e).start()


    def gram(row_side, wait, cols):
        high, low = split(row_side * (1.0 / (PEERS * EX_DEV)))
        row_side = jnp.concatenate([high, high, low, low], axis=0)
        wait()
        high, low = split(cols())
        col_side = jnp.concatenate([high, low, high, low], axis=0)
        out[...] = lax.dot_general(row_side, col_side, TN, preferred_element_type=F32)

    @pl.when(jnp.logical_not(lead))
    def _():
        wait_bytes(r_buf.at[pl.ds(0, (PEERS - 1) * PEERS)], recv_sem.at[3])
        gram(
            gather_rows(r_buf, PEERS, EX_DEV),
            lambda: wait_bytes(c_buf.at[pl.ds(0, (PEERS - 1) * PEERS)], recv_sem.at[4]),
            lambda: gather_rows(c_buf, EX_DEV, EX_DEV * PEERS),
        )

    @pl.when(lead)
    def _():
        def arrive(k):
            wait_bytes(lead_in.at[k, pl.ds(0, PEERS * PEERS - 1)], recv_sem.at[5 + k])

        arrive(0)
        gram(add_quarters(lead_in.at[0]), lambda: arrive(1), lambda: add_quarters(lead_in.at[1]))

    wait_bytes(part.at[pl.ds(0, PEERS - 1)], send_sem.at[0])
    wait_bytes(feat.at[pl.ds(0, PEERS - 1)], send_sem.at[1])
    wait_bytes(feat.at[pl.ds(0, PEERS - 1)], send_sem.at[2])

    @pl.when(meet != s)
    def _():
        wait_bytes(feat.at[0], send_sem.at[2])

    others = PEERS - (row_leads[1] - row_leads[0]) - jnp.where(lead, 0, 1)

    @pl.loop(0, others)
    def _(k):
        wait_bytes(own, send_sem.at[3])

    reached = PEERS - jnp.where(lead, 0, 1)
    for limits in LEADS:
        reached -= within(e, limits).astype(jnp.int32)

    @pl.loop(0, reached)
    def _(k):
        wait_bytes(at, send_sem.at[4])

    wait_bytes(lead_in.at[0, pl.ds(0, 2 * (sum(high - low for low, high in LEADS) - 1))], send_sem.at[5])

    @pl.when(jnp.logical_not(lead))
    def _():
        wait_bytes(lead_in.at[0, pl.ds(0, 2)], send_sem.at[5])


def shards(hidden, out_grad, lengths, left_signs, left_index, right_signs):
    tokens, ff = hidden.shape
    features = out_grad.shape[1]
    blocks = left_signs.shape[0]
    wide = EX_DEV * K2
    operands = (hidden, out_grad, right_signs, left_signs, left_index.T, lengths)
    return pl.pallas_call(
        functools.partial(exchange, blocks),
        out_shape=pltpu.VMEM((wide, wide), F32),
        in_specs=[pl.BlockSpec(memory_space=pltpu.HBM)] * 6,
        out_specs=pl.BlockSpec(memory_space=pltpu.VMEM),
        scratch_shapes=[
            pltpu.VMEM((EX_DEV, SEQ, ff), BF16),
            pltpu.VMEM((EX_DEV, SEQ, features), BF16),
            pltpu.VMEM((K2, features), BF16),
            pltpu.VMEM((blocks, 2, BK, BF), BF16),
            pltpu.SMEM((2, blocks), jnp.int32),
            pltpu.SMEM((EX_DEV,), jnp.int32),
            pltpu.VMEM((2 * K1, ff), BF16),
            pltpu.VMEM((PEERS, CHUNK, LANES), F32),
            pltpu.VMEM((PEERS, CHUNK, LANES), F32),
            pltpu.VMEM((PEERS, EX_DEV, K2), F32),
            pltpu.VMEM((PEERS, EX_DEV, K2), F32),
            pltpu.VMEM((EX_DEV, EX_DEV, EX_DEV, K2), F32),
            pltpu.VMEM((PEERS * PEERS, K2), F32),
            pltpu.VMEM((PEERS * PEERS, K2), F32),
            pltpu.VMEM((2, PEERS * PEERS, EX_DEV, K2), F32),
            pltpu.SemaphoreType.DMA((EX_DEV,)),
            pltpu.SemaphoreType.DMA((EX_DEV,)),
            pltpu.SemaphoreType.DMA((4,)),
            pltpu.SemaphoreType.DMA((6,)),
            pltpu.SemaphoreType.DMA((7,)),
            pltpu.SemaphoreType.REGULAR,
        ],
        compiler_params=pltpu.CompilerParams(
            collective_id=0, has_side_effects=True, vmem_limit_bytes=32 * 1024 * 1024
        ),
        name="exchange",
    )(*(pltpu.with_memory_space_constraint(a, pltpu.HBM) for a in operands))


def solution(mesh):
    in_specs = (
        P("ex", "slab"),
        P("ex", "slab"),
        P("ex"),
        P("slab", None, None, None),
        P("slab", None),
        P(None, "slab"),
    )
    out_specs = P("slab", "ex")
    return jax.shard_map(shards, mesh=mesh, in_specs=in_specs, out_specs=out_specs, check_vma=False)
```

```python
import functools

import jax
import jax.numpy as jnp
from jax import lax
from jax.experimental import pallas as pl
from jax.experimental.pallas import tpu as pltpu
from jax.sharding import PartitionSpec as P

D = 8192
FF = 28672
SEQ = 128
BF = 128
KB = 4
BK = 16
K2 = 128
K1 = 64
EX_DEV = 4
PEERS = 16
ZS = 8
Z_ORDER = (4, 3, 5, 2, 6, 1, 7)
Y_ORDER = (2, 3, 1, 0)
LEADS = ((1, 3), (0, 1), (0, 1), (0, 0), (0, 1))
X_ORDER = (2, 1, 3, 0)
COMPUTED = 1
TOK = SEQ // 4
CHUNK = TOK + TOK // 2
LANES = 128
HALF = LANES // 2
SCALE = FF**-0.5 * D**-0.5 * SEQ**-0.5

MESH = pl.DeviceIdType.MESH
F32 = jnp.float32
BF16 = jnp.bfloat16
NT = (((1,), (1,)), ((), ()))
TN = (((0,), (0,)), ((), ()))


def split(x):
    high = x.astype(BF16)
    return high, (x - high.astype(F32)).astype(BF16)


def remote(src, dst, send_sem, recv_sem, slab, ex):
    return pltpu.make_async_remote_copy(
        src_ref=src,
        dst_ref=dst,
        send_sem=send_sem,
        recv_sem=recv_sem,
        device_id=(slab, ex),
        device_id_type=MESH,
    )


def wait_bytes(ref, sem):
    pltpu.make_async_copy(ref, ref, sem).wait()


def gather_rows(ref, stride, step):
    planes = []
    for m in range(EX_DEV):
        rows = [ref[pl.ds(j * step + m, PEERS, stride=stride), :] for j in range(EX_DEV)]
        planes.append(jnp.concatenate(rows, axis=0))
    return jnp.concatenate(planes, axis=1)


def leads_of(slab):
    low = high = jnp.int32(0)
    for k, (first, last) in enumerate(LEADS):
        low = jnp.where(slab == k, first, low)
        high = jnp.where(slab == k, last, high)
    return low, high


def within(ex, limits):
    return jnp.logical_and(ex >= limits[0], ex < limits[1])


def add_quarters(ref):
    planes = [[] for _ in range(EX_DEV)]
    for j in range(EX_DEV):
        at = [ref[pl.ds((EX_DEV * j + q) * PEERS, PEERS)] for q in range(EX_DEV)]
        total = at[0] + at[1] + at[2] + at[3]
        for m in range(EX_DEV):
            planes[m].append(total[:, m])
    return jnp.concatenate([jnp.concatenate(rows, axis=0) for rows in planes], axis=1)


def exchange(
    blocks,
    hidden,
    out_grad,
    right,
    signs,
    index,
    lengths,
    out,
    hid_v,
    og_v,
    right_v,
    signs_v,
    index_v,
    lengths_v,
    left_v,
    part,
    part_in,
    feat,
    row_in,
    c_in,
    c_buf,
    r_buf,
    lead_in,
    hid_sem,
    og_sem,
    par_sem,
    send_sem,
    recv_sem,
    ready,
):
    s = lax.axis_index("slab")
    e = lax.axis_index("ex")
    y, x = lax.div(s, EX_DEV), lax.rem(s, EX_DEV)
    z, c = lax.div(e, 2), lax.rem(e, 2)

    row_leads = leads_of(s)
    lead = within(e, row_leads)

    barrier = pltpu.get_barrier_semaphore()
    for i in range(1, PEERS):
        pl.semaphore_signal(
            barrier, inc=1, device_id=(lax.rem(s + i, PEERS), e), device_id_type=MESH
        )

    @pl.loop(e + 1, PEERS)
    def _(to):
        pl.semaphore_signal(barrier, inc=1, device_id=(s, to), device_id_type=MESH)

    par = [
        pltpu.make_async_copy(signs, signs_v, par_sem.at[0]),
        pltpu.make_async_copy(index, index_v, par_sem.at[1]),
        pltpu.make_async_copy(lengths, lengths_v, par_sem.at[2]),
        pltpu.make_async_copy(right, right_v, par_sem.at[3]),
    ]
    for copy in par:
        copy.start()
    owners = [lax.rem(y + i, EX_DEV) for i in Y_ORDER]
    copies = []
    for i, j in enumerate(owners):
        rows = pl.ds(pl.multiple_of(j * SEQ, SEQ), SEQ)
        pair = (
            pltpu.make_async_copy(hidden.at[rows], hid_v.at[i], hid_sem.at[i]),
            pltpu.make_async_copy(out_grad.at[rows], og_v.at[i], og_sem.at[i]),
        )
        for copy in pair:
            copy.start()
        copies.append(pair)

    par[0].wait()
    par[1].wait()
    for r in range(blocks):
        pair = [signs_v[r, n].astype(F32) for n in range(2)]
        for k in range(KB):
            on = [(index_v[n, r] == k).astype(F32) for n in range(2)]
            dense = (pair[0] * on[0] + pair[1] * on[1]).astype(BF16)
            cols = pl.ds(r * BF, BF)
            left_v[pl.ds(k * BK, BK), cols] = dense
            left_v[pl.ds(K1 + k * BK, BK), cols] = dense
    par[2].wait()
    par[3].wait()

    token = lax.broadcasted_iota(jnp.int32, (SEQ, LANES), 0)
    first = lax.broadcasted_iota(jnp.int32, (TOK // 2, LANES), 1) < HALF
    for i, j in enumerate(owners):
        for copy in copies[i]:
            copy.wait()
        act = lax.dot_general(hid_v[i], left_v[...], NT, preferred_element_type=F32)
        act = jnp.where(token < lengths_v[j], act, 0.0)
        grad = lax.dot_general(og_v[i], right_v[...], NT, preferred_element_type=F32)
        for q in range(EX_DEV):
            at = i * EX_DEV + q
            t = q * TOK
            part[at, :TOK] = grad[t : t + TOK]
            part[at, TOK:] = jnp.where(first, act[t : t + TOK // 2], act[t + TOK // 2 : t + TOK])
        if i == COMPUTED:
            pl.semaphore_wait(barrier, PEERS - 1 + e)

            @pl.loop(0, e)
            def _(to):
                pl.semaphore_signal(ready, inc=1, device_id=(s, to), device_id_type=MESH)

        if i < COMPUTED:
            continue
        for n in range(i + 1) if i == COMPUTED else (i,):
            for k in X_ORDER:
                if Y_ORDER[n] == 0 and k == 0:
                    continue
                q = lax.rem(x + k, EX_DEV)
                remote(
                    part.at[n * EX_DEV + q],
                    part_in.at[s],
                    send_sem.at[0],
                    recv_sem.at[0],
                    owners[n] * EX_DEV + q,
                    e,
                ).start()

    part_in[s] = part[Y_ORDER.index(0) * EX_DEV + x]
    wait_bytes(part_in.at[pl.ds(0, PEERS - 1)], recv_sem.at[0])

    total = part_in[0]
    for i in range(1, PEERS):
        total += part_in[i]
    packed = total[TOK:]
    acts = jnp.concatenate([jnp.where(first, packed, 0.0), jnp.where(first, 0.0, packed)], axis=0)
    act_h, act_l = split(acts)
    grad_h, grad_l = split(total[:TOK])
    outer = lax.dot_general(
        jnp.concatenate([act_h, act_h, act_l, act_l], axis=0),
        jnp.concatenate([grad_h, grad_l, grad_h, grad_l], axis=0),
        TN,
        preferred_element_type=F32,
    )
    features = (outer[:K1] + outer[K1:]) * SCALE
    for i in range(PEERS):
        feat[i] = features[i * EX_DEV : (i + 1) * EX_DEV]

    def to_leads(slabs):
        for k in slabs:
            limits = LEADS[k]

            @pl.loop(*limits)
            def _(to):
                @pl.when(jnp.logical_or(s != k, e != to))
                def _():
                    for side, at in enumerate((k, to)):
                        remote(
                            feat.at[at],
                            lead_in.at[side, s * PEERS + e],
                            send_sem.at[5],
                            recv_sem.at[5 + side],
                            k,
                            to,
                        ).start()

    @pl.when(e >= PEERS // 2)
    def _():
        to_leads((0,))

    meet = y * EX_DEV + lax.rem(e, EX_DEV)
    spot = c_in.at[x, lax.div(e, EX_DEV)]

    def give(to):
        remote(feat.at[to], spot, send_sem.at[2], recv_sem.at[2], meet, to).start()

    pl.loop(0, e)(give)

    @pl.loop(1, PEERS)
    def _(i):
        to = lax.rem(s + i, PEERS)
        remote(feat.at[to], row_in.at[s], send_sem.at[1], recv_sem.at[1], to, e).start()


    @pl.when(e < PEERS - 1)
    def _():
        pl.semaphore_wait(ready, PEERS - 1 - e)

    pl.loop(e + 1, PEERS)(give)

    @pl.when(meet != s)
    def _():
        give(e)

    @pl.when(meet == s)
    def _():
        pltpu.make_async_copy(feat.at[e], spot, recv_sem.at[2]).start()

    @pl.when(e < PEERS // 2)
    def _():
        to_leads((0,))

    to_leads(range(1, len(LEADS)))

    @pl.when(lead)
    def _():
        lead_in[0, s * PEERS + e] = feat[s]
        lead_in[1, s * PEERS + e] = feat[e]

    row_in[s] = feat[s]
    wait_bytes(row_in.at[pl.ds(0, PEERS - 1)], recv_sem.at[1])
    rows = [
        row_in[4 * j] + row_in[4 * j + 1] + row_in[4 * j + 2] + row_in[4 * j + 3]
        for j in range(EX_DEV)
    ]
    slot = lax.rem(e, EX_DEV) * EX_DEV + lax.div(e, EX_DEV)
    own = r_buf.at[pl.ds(pl.multiple_of(slot * PEERS, PEERS), PEERS)]
    own[...] = jnp.concatenate(rows, axis=0)

    def pass_on(ex):
        @pl.when(jnp.logical_not(within(ex, row_leads)))
        def _():
            remote(own, own, send_sem.at[3], recv_sem.at[3], s, ex).start()

    for k in Z_ORDER:
        to = lax.rem(z + k, ZS) * 2
        pass_on(to + c)
        pass_on(to + 1 - c)
    pass_on(2 * z + 1 - c)

    wait_bytes(c_in, recv_sem.at[2])
    c_buf[pl.ds(pl.multiple_of(s * PEERS, PEERS), PEERS)] = jnp.concatenate(
        [c_in[0, i] + c_in[1, i] + c_in[2, i] + c_in[3, i] for i in range(EX_DEV)], axis=0
    )
    at = c_buf.at[pl.ds(pl.multiple_of(s * PEERS, PEERS), PEERS)]

    @pl.loop(1, PEERS)
    def _(i):
        to = lax.rem(s + i, PEERS)

        @pl.when(jnp.logical_not(within(e, leads_of(to))))
        def _():
            remote(at, at, send_sem.at[4], recv_sem.at[4], to, e).start()


    wait_bytes(part.at[pl.ds(0, PEERS - 1)], send_sem.at[0])
    wait_bytes(feat.at[pl.ds(0, PEERS - 1)], send_sem.at[1])
    wait_bytes(feat.at[pl.ds(0, PEERS - 1)], send_sem.at[2])

    @pl.when(meet != s)
    def _():
        wait_bytes(feat.at[0], send_sem.at[2])

    others = PEERS - (row_leads[1] - row_leads[0]) - jnp.where(lead, 0, 1)

    @pl.loop(0, others)
    def _(k):
        wait_bytes(own, send_sem.at[3])

    reached = PEERS - jnp.where(lead, 0, 1)
    for limits in LEADS:
        reached -= within(e, limits).astype(jnp.int32)

    @pl.loop(0, reached)
    def _(k):
        wait_bytes(at, send_sem.at[4])

    wait_bytes(lead_in.at[0, pl.ds(0, 2 * (sum(high - low for low, high in LEADS) - 1))], send_sem.at[5])

    @pl.when(jnp.logical_not(lead))
    def _():
        wait_bytes(lead_in.at[0, pl.ds(0, 2)], send_sem.at[5])

    def gram(row_side, wait, cols):
        high, low = split(row_side * (1.0 / (PEERS * EX_DEV)))
        row_side = jnp.concatenate([high, high, low, low], axis=0)
        wait()
        high, low = split(cols())
        col_side = jnp.concatenate([high, low, high, low], axis=0)
        out[...] = lax.dot_general(row_side, col_side, TN, preferred_element_type=F32)

    @pl.when(jnp.logical_not(lead))
    def _():
        wait_bytes(r_buf.at[pl.ds(0, (PEERS - 1) * PEERS)], recv_sem.at[3])
        gram(
            gather_rows(r_buf, PEERS, EX_DEV),
            lambda: wait_bytes(c_buf.at[pl.ds(0, (PEERS - 1) * PEERS)], recv_sem.at[4]),
            lambda: gather_rows(c_buf, EX_DEV, EX_DEV * PEERS),
        )

    @pl.when(lead)
    def _():
        def arrive(k):
            wait_bytes(lead_in.at[k, pl.ds(0, PEERS * PEERS - 1)], recv_sem.at[5 + k])

        arrive(0)
        gram(add_quarters(lead_in.at[0]), lambda: arrive(1), lambda: add_quarters(lead_in.at[1]))


def shards(hidden, out_grad, lengths, left_signs, left_index, right_signs):
    tokens, ff = hidden.shape
    features = out_grad.shape[1]
    blocks = left_signs.shape[0]
    wide = EX_DEV * K2
    operands = (hidden, out_grad, right_signs, left_signs, left_index.T, lengths)
    return pl.pallas_call(
        functools.partial(exchange, blocks),
        out_shape=pltpu.VMEM((wide, wide), F32),
        in_specs=[pl.BlockSpec(memory_space=pltpu.HBM)] * 6,
        out_specs=pl.BlockSpec(memory_space=pltpu.VMEM),
        scratch_shapes=[
            pltpu.VMEM((EX_DEV, SEQ, ff), BF16),
            pltpu.VMEM((EX_DEV, SEQ, features), BF16),
            pltpu.VMEM((K2, features), BF16),
            pltpu.VMEM((blocks, 2, BK, BF), BF16),
            pltpu.SMEM((2, blocks), jnp.int32),
            pltpu.SMEM((EX_DEV,), jnp.int32),
            pltpu.VMEM((2 * K1, ff), BF16),
            pltpu.VMEM((PEERS, CHUNK, LANES), F32),
            pltpu.VMEM((PEERS, CHUNK, LANES), F32),
            pltpu.VMEM((PEERS, EX_DEV, K2), F32),
            pltpu.VMEM((PEERS, EX_DEV, K2), F32),
            pltpu.VMEM((EX_DEV, EX_DEV, EX_DEV, K2), F32),
            pltpu.VMEM((PEERS * PEERS, K2), F32),
            pltpu.VMEM((PEERS * PEERS, K2), F32),
            pltpu.VMEM((2, PEERS * PEERS, EX_DEV, K2), F32),
            pltpu.SemaphoreType.DMA((EX_DEV,)),
            pltpu.SemaphoreType.DMA((EX_DEV,)),
            pltpu.SemaphoreType.DMA((4,)),
            pltpu.SemaphoreType.DMA((6,)),
            pltpu.SemaphoreType.DMA((7,)),
            pltpu.SemaphoreType.REGULAR,
        ],
        compiler_params=pltpu.CompilerParams(
            collective_id=0, has_side_effects=True, vmem_limit_bytes=32 * 1024 * 1024
        ),
        name="exchange",
    )(*(pltpu.with_memory_space_constraint(a, pltpu.HBM) for a in operands))


def solution(mesh):
    in_specs = (
        P("ex", "slab"),
        P("ex", "slab"),
        P("ex"),
        P("slab", None, None, None),
        P("slab", None),
        P(None, "slab"),
    )
    out_specs = P("slab", "ex")
    return jax.shard_map(shards, mesh=mesh, in_specs=in_specs, out_specs=out_specs, check_vma=False)
```

```python
import functools

import jax
import jax.numpy as jnp
from jax import lax
from jax.experimental import pallas as pl
from jax.experimental.pallas import tpu as pltpu
from jax.sharding import PartitionSpec as P

D = 8192
FF = 28672
SEQ = 128
BF = 128
KB = 4
BK = 16
K2 = 128
K1 = 64
EX_DEV = 4
PEERS = 16
ZS = 8
Z_ORDER = (4, 5, 3, 6, 2, 7, 1)
Y_ORDER = (2, 3, 1, 0)
LEADS = ((1, 3), (0, 1), (0, 1), (0, 0), (0, 1))
X_ORDER = (2, 1, 3, 0)
COMPUTED = 1
TOK = SEQ // 4
CHUNK = TOK + TOK // 2
LANES = 128
HALF = LANES // 2
SCALE = FF**-0.5 * D**-0.5 * SEQ**-0.5

MESH = pl.DeviceIdType.MESH
F32 = jnp.float32
BF16 = jnp.bfloat16
NT = (((1,), (1,)), ((), ()))
TN = (((0,), (0,)), ((), ()))


def split(x):
    high = x.astype(BF16)
    return high, (x - high.astype(F32)).astype(BF16)


def remote(src, dst, send_sem, recv_sem, slab, ex):
    return pltpu.make_async_remote_copy(
        src_ref=src,
        dst_ref=dst,
        send_sem=send_sem,
        recv_sem=recv_sem,
        device_id=(slab, ex),
        device_id_type=MESH,
    )


def wait_bytes(ref, sem):
    pltpu.make_async_copy(ref, ref, sem).wait()


def gather_rows(ref, stride, step):
    planes = []
    for m in range(EX_DEV):
        rows = [ref[pl.ds(j * step + m, PEERS, stride=stride), :] for j in range(EX_DEV)]
        planes.append(jnp.concatenate(rows, axis=0))
    return jnp.concatenate(planes, axis=1)


def leads_of(slab):
    low = high = jnp.int32(0)
    for k, (first, last) in enumerate(LEADS):
        low = jnp.where(slab == k, first, low)
        high = jnp.where(slab == k, last, high)
    return low, high


def within(ex, limits):
    return jnp.logical_and(ex >= limits[0], ex < limits[1])


def add_quarters(ref):
    planes = [[] for _ in range(EX_DEV)]
    for j in range(EX_DEV):
        at = [ref[pl.ds((EX_DEV * j + q) * PEERS, PEERS)] for q in range(EX_DEV)]
        total = at[0] + at[1] + at[2] + at[3]
        for m in range(EX_DEV):
            planes[m].append(total[:, m])
    return jnp.concatenate([jnp.concatenate(rows, axis=0) for rows in planes], axis=1)


def exchange(
    blocks,
    hidden,
    out_grad,
    right,
    signs,
    index,
    lengths,
    out,
    hid_v,
    og_v,
    right_v,
    signs_v,
    index_v,
    lengths_v,
    left_v,
    part,
    part_in,
    feat,
    row_in,
    c_in,
    c_buf,
    r_buf,
    lead_in,
    hid_sem,
    og_sem,
    par_sem,
    send_sem,
    recv_sem,
    ready,
):
    s = lax.axis_index("slab")
    e = lax.axis_index("ex")
    y, x = lax.div(s, EX_DEV), lax.rem(s, EX_DEV)
    z, c = lax.div(e, 2), lax.rem(e, 2)

    row_leads = leads_of(s)
    lead = within(e, row_leads)

    barrier = pltpu.get_barrier_semaphore()
    for i in range(1, PEERS):
        pl.semaphore_signal(
            barrier, inc=1, device_id=(lax.rem(s + i, PEERS), e), device_id_type=MESH
        )

    @pl.loop(e + 1, PEERS)
    def _(to):
        pl.semaphore_signal(barrier, inc=1, device_id=(s, to), device_id_type=MESH)

    par = [
        pltpu.make_async_copy(signs, signs_v, par_sem.at[0]),
        pltpu.make_async_copy(index, index_v, par_sem.at[1]),
        pltpu.make_async_copy(lengths, lengths_v, par_sem.at[2]),
        pltpu.make_async_copy(right, right_v, par_sem.at[3]),
    ]
    for copy in par:
        copy.start()
    owners = [lax.rem(y + i, EX_DEV) for i in Y_ORDER]
    copies = []
    for i, j in enumerate(owners):
        rows = pl.ds(pl.multiple_of(j * SEQ, SEQ), SEQ)
        pair = (
            pltpu.make_async_copy(hidden.at[rows], hid_v.at[i], hid_sem.at[i]),
            pltpu.make_async_copy(out_grad.at[rows], og_v.at[i], og_sem.at[i]),
        )
        for copy in pair:
            copy.start()
        copies.append(pair)

    par[0].wait()
    par[1].wait()
    for r in range(blocks):
        pair = [signs_v[r, n].astype(F32) for n in range(2)]
        for k in range(KB):
            on = [(index_v[n, r] == k).astype(F32) for n in range(2)]
            dense = (pair[0] * on[0] + pair[1] * on[1]).astype(BF16)
            cols = pl.ds(r * BF, BF)
            left_v[pl.ds(k * BK, BK), cols] = dense
            left_v[pl.ds(K1 + k * BK, BK), cols] = dense
    par[2].wait()
    par[3].wait()

    token = lax.broadcasted_iota(jnp.int32, (SEQ, LANES), 0)
    first = lax.broadcasted_iota(jnp.int32, (TOK // 2, LANES), 1) < HALF
    for i, j in enumerate(owners):
        for copy in copies[i]:
            copy.wait()
        act = lax.dot_general(hid_v[i], left_v[...], NT, preferred_element_type=F32)
        act = jnp.where(token < lengths_v[j], act, 0.0)
        grad = lax.dot_general(og_v[i], right_v[...], NT, preferred_element_type=F32)
        for q in range(EX_DEV):
            at = i * EX_DEV + q
            t = q * TOK
            part[at, :TOK] = grad[t : t + TOK]
            part[at, TOK:] = jnp.where(first, act[t : t + TOK // 2], act[t + TOK // 2 : t + TOK])
        if i == COMPUTED:
            pl.semaphore_wait(barrier, PEERS - 1 + e)

            @pl.loop(0, e)
            def _(to):
                pl.semaphore_signal(ready, inc=1, device_id=(s, to), device_id_type=MESH)

        if i < COMPUTED:
            continue
        for n in range(i + 1) if i == COMPUTED else (i,):
            for k in X_ORDER:
                if Y_ORDER[n] == 0 and k == 0:
                    continue
                q = lax.rem(x + k, EX_DEV)
                remote(
                    part.at[n * EX_DEV + q],
                    part_in.at[s],
                    send_sem.at[0],
                    recv_sem.at[0],
                    owners[n] * EX_DEV + q,
                    e,
                ).start()

    part_in[s] = part[Y_ORDER.index(0) * EX_DEV + x]
    wait_bytes(part_in.at[pl.ds(0, PEERS - 1)], recv_sem.at[0])

    total = part_in[0]
    for i in range(1, PEERS):
        total += part_in[i]
    packed = total[TOK:]
    acts = jnp.concatenate([jnp.where(first, packed, 0.0), jnp.where(first, 0.0, packed)], axis=0)
    act_h, act_l = split(acts)
    grad_h, grad_l = split(total[:TOK])
    outer = lax.dot_general(
        jnp.concatenate([act_h, act_h, act_l, act_l], axis=0),
        jnp.concatenate([grad_h, grad_l, grad_h, grad_l], axis=0),
        TN,
        preferred_element_type=F32,
    )
    features = (outer[:K1] + outer[K1:]) * SCALE
    for i in range(PEERS):
        feat[i] = features[i * EX_DEV : (i + 1) * EX_DEV]

    def to_leads(slabs):
        for k in slabs:
            limits = LEADS[k]

            @pl.loop(*limits)
            def _(to):
                @pl.when(jnp.logical_or(s != k, e != to))
                def _():
                    for side, at in enumerate((k, to)):
                        remote(
                            feat.at[at],
                            lead_in.at[side, s * PEERS + e],
                            send_sem.at[5],
                            recv_sem.at[5 + side],
                            k,
                            to,
                        ).start()

    meet = y * EX_DEV + lax.rem(e, EX_DEV)
    spot = c_in.at[x, lax.div(e, EX_DEV)]

    def give(to):
        remote(feat.at[to], spot, send_sem.at[2], recv_sem.at[2], meet, to).start()

    pl.loop(0, e)(give)

    @pl.when(e >= PEERS // 2)
    def _():
        to_leads((0,))

    @pl.loop(1, PEERS)
    def _(i):
        to = lax.rem(s + i, PEERS)
        remote(feat.at[to], row_in.at[s], send_sem.at[1], recv_sem.at[1], to, e).start()


    @pl.when(e < PEERS - 1)
    def _():
        pl.semaphore_wait(ready, PEERS - 1 - e)

    pl.loop(e + 1, PEERS)(give)

    @pl.when(meet != s)
    def _():
        give(e)

    @pl.when(meet == s)
    def _():
        pltpu.make_async_copy(feat.at[e], spot, recv_sem.at[2]).start()

    @pl.when(e < PEERS // 2)
    def _():
        to_leads((0,))

    to_leads(range(1, len(LEADS)))

    @pl.when(lead)
    def _():
        lead_in[0, s * PEERS + e] = feat[s]
        lead_in[1, s * PEERS + e] = feat[e]

    row_in[s] = feat[s]
    wait_bytes(row_in.at[pl.ds(0, PEERS - 1)], recv_sem.at[1])
    rows = [
        row_in[4 * j] + row_in[4 * j + 1] + row_in[4 * j + 2] + row_in[4 * j + 3]
        for j in range(EX_DEV)
    ]
    slot = lax.rem(e, EX_DEV) * EX_DEV + lax.div(e, EX_DEV)
    own = r_buf.at[pl.ds(pl.multiple_of(slot * PEERS, PEERS), PEERS)]
    own[...] = jnp.concatenate(rows, axis=0)

    def pass_on(ex):
        @pl.when(jnp.logical_not(within(ex, row_leads)))
        def _():
            remote(own, own, send_sem.at[3], recv_sem.at[3], s, ex).start()

    for k in Z_ORDER:
        to = lax.rem(z + k, ZS) * 2
        pass_on(to + c)
        pass_on(to + 1 - c)
    pass_on(2 * z + 1 - c)

    wait_bytes(c_in, recv_sem.at[2])
    c_buf[pl.ds(pl.multiple_of(s * PEERS, PEERS), PEERS)] = jnp.concatenate(
        [c_in[0, i] + c_in[1, i] + c_in[2, i] + c_in[3, i] for i in range(EX_DEV)], axis=0
    )
    at = c_buf.at[pl.ds(pl.multiple_of(s * PEERS, PEERS), PEERS)]

    @pl.loop(1, PEERS)
    def _(i):
        to = lax.rem(s + i, PEERS)

        @pl.when(jnp.logical_not(within(e, leads_of(to))))
        def _():
            remote(at, at, send_sem.at[4], recv_sem.at[4], to, e).start()


    wait_bytes(part.at[pl.ds(0, PEERS - 1)], send_sem.at[0])
    wait_bytes(feat.at[pl.ds(0, PEERS - 1)], send_sem.at[1])
    wait_bytes(feat.at[pl.ds(0, PEERS - 1)], send_sem.at[2])

    @pl.when(meet != s)
    def _():
        wait_bytes(feat.at[0], send_sem.at[2])

    others = PEERS - (row_leads[1] - row_leads[0]) - jnp.where(lead, 0, 1)

    @pl.loop(0, others)
    def _(k):
        wait_bytes(own, send_sem.at[3])

    reached = PEERS - jnp.where(lead, 0, 1)
    for limits in LEADS:
        reached -= within(e, limits).astype(jnp.int32)

    @pl.loop(0, reached)
    def _(k):
        wait_bytes(at, send_sem.at[4])

    wait_bytes(lead_in.at[0, pl.ds(0, 2 * (sum(high - low for low, high in LEADS) - 1))], send_sem.at[5])

    @pl.when(jnp.logical_not(lead))
    def _():
        wait_bytes(lead_in.at[0, pl.ds(0, 2)], send_sem.at[5])

    def gram(row_side, wait, cols):
        high, low = split(row_side * (1.0 / (PEERS * EX_DEV)))
        row_side = jnp.concatenate([high, high, low, low], axis=0)
        wait()
        high, low = split(cols())
        col_side = jnp.concatenate([high, low, high, low], axis=0)
        out[...] = lax.dot_general(row_side, col_side, TN, preferred_element_type=F32)

    @pl.when(jnp.logical_not(lead))
    def _():
        wait_bytes(r_buf.at[pl.ds(0, (PEERS - 1) * PEERS)], recv_sem.at[3])
        gram(
            gather_rows(r_buf, PEERS, EX_DEV),
            lambda: wait_bytes(c_buf.at[pl.ds(0, (PEERS - 1) * PEERS)], recv_sem.at[4]),
            lambda: gather_rows(c_buf, EX_DEV, EX_DEV * PEERS),
        )

    @pl.when(lead)
    def _():
        def arrive(k):
            wait_bytes(lead_in.at[k, pl.ds(0, PEERS * PEERS - 1)], recv_sem.at[5 + k])

        arrive(0)
        gram(add_quarters(lead_in.at[0]), lambda: arrive(1), lambda: add_quarters(lead_in.at[1]))


def shards(hidden, out_grad, lengths, left_signs, left_index, right_signs):
    tokens, ff = hidden.shape
    features = out_grad.shape[1]
    blocks = left_signs.shape[0]
    wide = EX_DEV * K2
    operands = (hidden, out_grad, right_signs, left_signs, left_index.T, lengths)
    return pl.pallas_call(
        functools.partial(exchange, blocks),
        out_shape=pltpu.VMEM((wide, wide), F32),
        in_specs=[pl.BlockSpec(memory_space=pltpu.HBM)] * 6,
        out_specs=pl.BlockSpec(memory_space=pltpu.VMEM),
        scratch_shapes=[
            pltpu.VMEM((EX_DEV, SEQ, ff), BF16),
            pltpu.VMEM((EX_DEV, SEQ, features), BF16),
            pltpu.VMEM((K2, features), BF16),
            pltpu.VMEM((blocks, 2, BK, BF), BF16),
            pltpu.SMEM((2, blocks), jnp.int32),
            pltpu.SMEM((EX_DEV,), jnp.int32),
            pltpu.VMEM((2 * K1, ff), BF16),
            pltpu.VMEM((PEERS, CHUNK, LANES), F32),
            pltpu.VMEM((PEERS, CHUNK, LANES), F32),
            pltpu.VMEM((PEERS, EX_DEV, K2), F32),
            pltpu.VMEM((PEERS, EX_DEV, K2), F32),
            pltpu.VMEM((EX_DEV, EX_DEV, EX_DEV, K2), F32),
            pltpu.VMEM((PEERS * PEERS, K2), F32),
            pltpu.VMEM((PEERS * PEERS, K2), F32),
            pltpu.VMEM((2, PEERS * PEERS, EX_DEV, K2), F32),
            pltpu.SemaphoreType.DMA((EX_DEV,)),
            pltpu.SemaphoreType.DMA((EX_DEV,)),
            pltpu.SemaphoreType.DMA((4,)),
            pltpu.SemaphoreType.DMA((6,)),
            pltpu.SemaphoreType.DMA((7,)),
            pltpu.SemaphoreType.REGULAR,
        ],
        compiler_params=pltpu.CompilerParams(
            collective_id=0, has_side_effects=True, vmem_limit_bytes=32 * 1024 * 1024
        ),
        name="exchange",
    )(*(pltpu.with_memory_space_constraint(a, pltpu.HBM) for a in operands))


def solution(mesh):
    in_specs = (
        P("ex", "slab"),
        P("ex", "slab"),
        P("ex"),
        P("slab", None, None, None),
        P("slab", None),
        P(None, "slab"),
    )
    out_specs = P("slab", "ex")
    return jax.shard_map(shards, mesh=mesh, in_specs=in_specs, out_specs=out_specs, check_vma=False)
```
